32 devices in a mesh: groups: 2 (over y), space: 4 (over z), feat: 2 (over x), edge: 2 (over core).
Axes of the slice: x: 2, y: 2, z: 4, core: 2. Of those that a mesh axis runs over, the one named last changes fastest.
Arguments:
- grid_latent: bfloat16 [32768, 512], P(('groups', 'space', 'edge'), 'feat'), parts along dimension 0, may hold values from -6 to 6
- enc_weight: bfloat16 [512, 512], P(None, 'feat'), may hold values from -0.25 to 0.25
- mesh_latent: bfloat16 [10240, 512], P(('groups', 'space', 'edge'), 'feat'), parts along dimension 0, may hold values from -6 to 6
- g2m_src: int32 [16, 7, 256], P(('groups', 'space', 'edge')), parts along dimension 0, may hold values from 0 to 2047
- g2m_dst: int32 [16, 7, 256], P(('groups', 'space', 'edge')), parts along dimension 0, may hold values from 0 to 640, as said below
- g2m_coef: float32 [16, 7, 256], P(('groups', 'space', 'edge')), parts along dimension 0, may hold values from 0.2 to 0.6
- src_weights: bfloat16 [2, 512, 512], P(None, None, 'feat'), may hold values from -0.25 to 0.25
- dst_weights: bfloat16 [2, 512, 512], P(None, None, 'feat'), may hold values from -0.25 to 0.25
- halo_send: int32 [16, 6, 64], P(('groups', 'space', 'edge')), parts along dimension 0, may hold values from 0 to 639
- m2m_src: int32 [16, 5120], P(('groups', 'space', 'edge')), parts along dimension 0, may hold values from 0 to 1023, as said below
- m2m_dst: int32 [16, 5120], P(('groups', 'space', 'edge')), parts along dimension 0, may hold values from 0 to 639
- m2m_coef: float32 [16, 5120], P(('groups', 'space', 'edge')), parts along dimension 0, may hold values from 0.15 to 0.5
Outputs:
- mesh_state: bfloat16 [10240, 512], P(('groups', 'space', 'edge'), 'feat'), parts along dimension 0
The draws below stay inside these ranges and needn't reach their ends.
There are 2 independent parts, one for each index of `groups`. The reference program is written for one: setup_inputs(seed, part) draws one part's arguments, and reference() takes and returns one part's arrays. A program takes and returns all parts, laid end to end along the dimension named above; an argument that names none is the same for every part. Nothing has to cross between parts.
Inputs may be any that keep to these rules, and one draw needn't show every extreme that they name: `g2m_dst`: block j of region half s goes to owner s + j - 3. In each block the used slots come first and hold local mesh rows of that owner; the others hold 640. Blocks whose owner lies outside the region halves hold only 640; every other block has at least one used slot, the own block (3) is full, and some owner receives 256 used slots from each of its 7 senders. `m2m_src`: A listed block whose region half p lies outside the region halves is never named; every other value from 640 up appears in each region half's row.
All inputs are finite; a program needn't handle non-finite values.
Results may differ from the reference program's by a relative error of at most 0.012.
Values may be sent and summed in bfloat16 or wider, within the bound.
No kernel may reach another device: no remote copies, remote signals or barrier semaphores. Data moves between devices by JAX's collectives and lax.ppermute only.
A program may use at most 128 MiB of HBM per device.

```python
import jax
import jax.numpy as jnp

D = 512
G_DEV = 2048
M_DEV = 640
CAP = 256
HCAP = 64
REACH = 3
STEPS = 2
BLOCKS = 7
LINKS = 6
SHARDS = 8
ME_DEV = 5120
GRID = 16384
MESH = 5120


def draw_g2m_dst(key, part):
    key = jax.random.fold_in(key, 3)
    count_key, hot_key, row_key = jax.random.split(key, 3)
    counts = jax.random.randint(count_key, (SHARDS, BLOCKS), 1, CAP + 1)
    offsets = jnp.arange(BLOCKS) - REACH
    destination = jnp.arange(SHARDS)[:, None] + offsets[None, :]
    hottest = jax.random.randint(hot_key, (), REACH, SHARDS - REACH)
    counts = jnp.where(destination == hottest, CAP, counts)
    counts = jnp.where(offsets[None, :] == 0, CAP, counts)
    counts = jnp.where((destination >= 0) & (destination < SHARDS), counts, 0)
    filled = jnp.arange(CAP)[None, None, :] < counts[:, :, None]
    mesh_rows = jax.random.randint(row_key, (SHARDS, BLOCKS, CAP), 0, M_DEV)
    return jnp.where(filled, mesh_rows, M_DEV).astype(jnp.int32)


def draw_g2m_src(key, part):
    key = jax.random.fold_in(key, 7)
    return jax.random.randint(key, (SHARDS, BLOCKS, CAP), 0, G_DEV).astype(jnp.int32)


def draw_m2m_src(key, part):
    key = jax.random.fold_in(key, 5)
    local_key, spare_key, order_key = jax.random.split(key, 3)
    listed = M_DEV + jnp.broadcast_to(jnp.arange(LINKS * HCAP, dtype=jnp.int32), (SHARDS, LINKS * HCAP))
    link_offsets = jnp.concatenate([jnp.arange(-REACH, 0), jnp.arange(1, REACH + 1)])
    source = jnp.arange(SHARDS)[:, None] - link_offsets[None, :]
    present = (source >= 0) & (source < SHARDS)
    present = jnp.repeat(present, HCAP, axis=1)
    spare = jax.random.randint(spare_key, (SHARDS, LINKS * HCAP), 0, M_DEV).astype(jnp.int32)
    listed = jnp.where(present, listed, spare)
    local_rows = jax.random.randint(local_key, (SHARDS, ME_DEV - LINKS * HCAP), 0, M_DEV).astype(jnp.int32)
    joined = jnp.concatenate([listed, local_rows], axis=1)
    orders = jax.vmap(lambda single: jax.random.permutation(single, ME_DEV))(jax.random.split(order_key, SHARDS))
    return jnp.take_along_axis(joined, orders, axis=1).astype(jnp.int32)


def place_ends(drawn, own_key, low, largest):
    longest = drawn.shape.index(max(drawn.shape))
    spots = []
    for shift in (0, 1):
        where = [jax.random.randint(jax.random.fold_in(own_key, axis), (), 0, length) for axis, length in enumerate(drawn.shape)]
        where[longest] = (where[longest] + shift) % drawn.shape[longest]
        spots.append(tuple(where))
    return drawn.at[spots[0]].set(low).at[spots[1]].set(largest)


def levels(key, extent, pieces, smallest, top_value):
    def one(position, blocks):
        steps = jax.random.uniform(jax.random.fold_in(jax.random.fold_in(key, 6), position), (blocks,), jnp.float32, smallest / len(pieces), top_value / len(pieces))
        return jnp.repeat(jnp.exp(steps), extent[position] // blocks).reshape((-1,) + (1,) * (len(extent) - position - 1))

    level = one(*pieces[0])
    for cut in pieces[1:]:
        level = level * one(*cut)
    return level


def bell_draw(stream_key, dims, scale, reach, cuts=(), held_as=jnp.bfloat16):
    drawn = scale * jax.random.normal(stream_key, dims, jnp.float32)
    if cuts:
        drawn = drawn * levels(stream_key, dims, cuts, -0.22, 0.18)
    return jnp.clip(drawn, -reach, reach).astype(held_as)


def setup_inputs(seed: int = 0, part: int = 0) -> dict:
    splits = jax.random.split(jax.random.key(seed), 13)
    own_keys = jax.random.split(jax.random.fold_in(splits[12], part), 13)
    grid_latent = bell_draw(own_keys[0], (GRID, D), 1.0, 6.0, ((0, 8), (1, 2)))
    enc_weight = bell_draw(splits[1], (D, D), D ** -0.5, 0.25, ((1, 2),))
    mesh_latent = bell_draw(own_keys[2], (MESH, D), 1.0, 6.0, ((0, 8), (1, 2)))
    g2m_src = draw_g2m_src(jax.random.fold_in(jax.random.fold_in(splits[12], part), 71), part)
    g2m_dst = draw_g2m_dst(jax.random.fold_in(jax.random.fold_in(splits[12], part), 71), part)
    g2m_coef = jnp.clip(0.2 + 0.400000021 * jax.random.uniform(own_keys[5], (SHARDS, BLOCKS, CAP), jnp.float32) ** levels(own_keys[5], (SHARDS, BLOCKS, CAP), ((0, 8),), -0.2, 0.2), 0.2, 0.6)
    src_weights = bell_draw(splits[6], (STEPS, D, D), D ** -0.5, 0.25, ((2, 2),))
    dst_weights = bell_draw(splits[7], (STEPS, D, D), D ** -0.5, 0.25, ((2, 2),))
    halo_send = place_ends(jax.random.randint(own_keys[8], (SHARDS, LINKS, HCAP), 0, M_DEV), jax.random.fold_in(own_keys[8], 1), 0, M_DEV - 1).astype(jnp.int32)
    m2m_src = draw_m2m_src(jax.random.fold_in(jax.random.fold_in(splits[12], part), 71), part)
    m2m_dst = place_ends(jax.random.randint(own_keys[10], (SHARDS, ME_DEV), 0, M_DEV), jax.random.fold_in(own_keys[10], 1), 0, M_DEV - 1).astype(jnp.int32)
    m2m_coef = jnp.clip(0.15 + 0.35 * jax.random.uniform(own_keys[11], (SHARDS, ME_DEV), jnp.float32) ** levels(own_keys[11], (SHARDS, ME_DEV), ((0, 8),), -0.2, 0.2), 0.15, 0.5)
    return dict(grid_latent=grid_latent, enc_weight=enc_weight, mesh_latent=mesh_latent, g2m_src=g2m_src, g2m_dst=g2m_dst, g2m_coef=g2m_coef, src_weights=src_weights, dst_weights=dst_weights, halo_send=halo_send, m2m_src=m2m_src, m2m_dst=m2m_dst, m2m_coef=m2m_coef)


def aggregate(values, targets, count):
    return jax.ops.segment_sum(values, targets, num_segments=count + 1)[:count]


def reference(grid_latent, enc_weight, mesh_latent, g2m_src, g2m_dst, g2m_coef, src_weights, dst_weights, halo_send, m2m_src, m2m_dst, m2m_coef):
    projected = jnp.dot(grid_latent, enc_weight, preferred_element_type=jnp.float32)
    owners = jnp.arange(SHARDS, dtype=jnp.int32)
    offsets = jnp.arange(BLOCKS, dtype=jnp.int32) - REACH
    grid_rows = (owners[:, None, None] * G_DEV + g2m_src).reshape(-1)
    edge_scale = g2m_coef.reshape(-1, 1).astype(jnp.float32)
    encoded = (edge_scale * jax.nn.silu(projected[grid_rows])).astype(jnp.bfloat16)
    destination = owners[:, None] + offsets[None, :]
    inside = (destination >= 0) & (destination < SHARDS)
    used = inside[:, :, None] & (g2m_dst < M_DEV)
    mesh_rows = jnp.where(used, destination[:, :, None] * M_DEV + g2m_dst, SHARDS * M_DEV).astype(jnp.int32).reshape(-1)
    gathered_in = aggregate(encoded.astype(jnp.float32), mesh_rows, SHARDS * M_DEV)
    state = (mesh_latent.astype(jnp.float32) + gathered_in).astype(jnp.bfloat16)
    link_offsets = jnp.concatenate([jnp.arange(-REACH, 0, dtype=jnp.int32), jnp.arange(1, REACH + 1, dtype=jnp.int32)])
    source = jnp.clip(owners[:, None] - link_offsets[None, :], 0, SHARDS - 1).astype(jnp.int32)
    columns = jnp.arange(LINKS, dtype=jnp.int32)[None, :]
    listed = source[:, :, None] * M_DEV + halo_send[source, columns]
    listed = listed.reshape(SHARDS, LINKS * HCAP).astype(jnp.int32)
    own_rows = owners[:, None] * M_DEV + jnp.arange(M_DEV, dtype=jnp.int32)[None, :]
    extended = jnp.concatenate([own_rows, listed], axis=1)
    senders = jnp.take_along_axis(extended, m2m_src, axis=1).reshape(-1)
    receivers = (owners[:, None] * M_DEV + m2m_dst).reshape(-1)
    mesh_scale = m2m_coef.reshape(-1, 1).astype(jnp.float32)
    for layer in range(STEPS):
        sender = jnp.dot(state, src_weights[layer], preferred_element_type=jnp.float32).astype(jnp.bfloat16)
        receiver = jnp.dot(state, dst_weights[layer], preferred_element_type=jnp.float32)
        message = (mesh_scale * jax.nn.silu(sender[senders].astype(jnp.float32) + receiver[receivers])).astype(jnp.bfloat16)
        update = aggregate(message.astype(jnp.float32), receivers, SHARDS * M_DEV)
        state = (state.astype(jnp.float32) + update).astype(jnp.bfloat16)
    return state
```

```python
import functools

import jax
import jax.numpy as jnp
from jax import lax
from jax.experimental import pallas as pl
from jax.experimental.pallas import tpu as pltpu
from jax.sharding import PartitionSpec as P

REGION = ("space", "edge")
PAD = 16
VMEM_BYTES = 56 * 1024 * 1024


def params():
    return pltpu.CompilerParams(vmem_limit_bytes=VMEM_BYTES)


def vmem_specs(count):
    return [pl.BlockSpec(memory_space=pltpu.VMEM)] * count


def passed_along(value, steps):
    count = lax.axis_size(REGION)
    first, last = (max(0, -steps), min(count, count - steps))
    return lax.ppermute(value, REGION, [(i, i + steps) for i in range(first, last)])


def from_others(value):
    n = lax.axis_size("feat")
    return [
        lax.ppermute(value, "feat", [(i, (i + k) % n) for i in range(n)]) for k in range(1, n)
    ]


def own_and_others_rows(weight_ref, channels, others):
    n = others + 1
    me = lax.axis_index("feat")
    blocks = []
    for k in range(n):
        owner = lax.rem(me - k + n, n)
        start = pl.multiple_of(owner * channels, channels)
        blocks.append(weight_ref[0, pl.ds(start, channels), :])
    return blocks


def silu(v):
    half = 0.5 * v
    return half + half * jnp.tanh(half)


def column(row):
    length = row.shape[1]
    parts = [
        jnp.broadcast_to(row[:, c * 128 : (c + 1) * 128], (128, 128)).T for c in range(length // 128)
    ]
    return parts[0] if len(parts) == 1 else jnp.concatenate(parts, axis=0)


def lane_iota(count):
    return lax.broadcasted_iota(jnp.int32, (16, count), 1).astype(jnp.int16)


def row_iota(count):
    return lax.broadcasted_iota(jnp.int32, (count, 128), 0).astype(jnp.int16)


def tiled(value, rows, lanes):
    if value.shape[0] != rows:
        value = jnp.concatenate([value] * (rows // value.shape[0]), axis=0)
    if value.shape[1] != lanes:
        value = jnp.concatenate([value] * (lanes // value.shape[1]), axis=1)
    return value


def pick_mask(column16, lane16):
    rows, lanes = (column16.shape[0], lane16.shape[1])
    same = tiled(column16, rows, lanes) == tiled(lane16, rows, lanes)
    return jnp.where(same, jnp.bfloat16(1), jnp.bfloat16(0))


def sum_mask(row, rows16, scale=None):
    count, length = (rows16.shape[0], row.shape[1])
    targets = jnp.broadcast_to(row, (16, length)).astype(jnp.int16)
    same = tiled(rows16, count, length) == tiled(targets, count, length)
    if scale is None:
        here = jnp.bfloat16(1)
    else:
        here = tiled(jnp.broadcast_to(scale, (16, length)).astype(jnp.bfloat16), count, length)
    return jnp.where(same, here, jnp.bfloat16(0))


def dot(a, b):
    return jnp.dot(a, b, preferred_element_type=jnp.float32)


def pick_kernel(order, index_ref, table_ref, out_ref):
    lanes = lane_iota(table_ref.shape[0])
    for place, j in enumerate(order):
        col = column(index_ref[0, pl.ds(j, 1), :]).astype(jnp.int16)
        out_ref[place] = dot(pick_mask(col, lanes), table_ref[...]).astype(jnp.bfloat16)


def pick(order, g2m_src, grid_latent):
    capacity = g2m_src.shape[2]
    rows, channels = grid_latent.shape
    return pl.pallas_call(
        functools.partial(pick_kernel, order),
        out_shape=jax.ShapeDtypeStruct((len(order), capacity, channels), jnp.bfloat16),
        in_specs=vmem_specs(2),
        out_specs=pl.BlockSpec(memory_space=pltpu.VMEM),
        compiler_params=params(),
        cost_estimate=pl.CostEstimate(
            flops=2 * len(order) * capacity * rows * channels,
            bytes_accessed=2 * (rows + len(order) * capacity) * channels,
            transcendentals=0,
        ),
    )(g2m_src, grid_latent)


def encode_kernel(order, others, weight_ref, coef_ref, target_ref, *refs):
    sources, outs = (refs[: others + 1], refs[others + 1 :])
    capacity, channels = sources[0].shape[1:]
    weights = own_and_others_rows(weight_ref, channels, others)
    line = lax.broadcasted_iota(jnp.int32, (PAD, channels), 0)
    pieces = capacity // channels
    for place, j in enumerate(order):
        projected = dot(sources[0][place], weights[0])
        for source, weight in zip(sources[1:], weights[1:]):
            projected += dot(source[place], weight)
        scale = tiled(column(coef_ref[0, pl.ds(j, 1), :]), capacity, channels)
        outs[place][pl.ds(0, capacity), :] = (scale * silu(projected)).astype(jnp.bfloat16)
        target = target_ref[0, pl.ds(j, 1), :]
        code = jnp.zeros((PAD, channels), jnp.float32)
        for number, part in enumerate((target >> 3, target & 7)):
            part = part.astype(jnp.float32)
            for piece in range(pieces):
                values = part[:, piece * channels : (piece + 1) * channels]
                code = jnp.where(line == number * pieces + piece, values, code)
        outs[place][pl.ds(capacity, PAD), :] = code.astype(jnp.bfloat16)


def encode(order, picked, arrived, enc_weight, g2m_coef, g2m_dst):
    count, capacity, channels = picked.shape
    sent = jax.ShapeDtypeStruct((capacity + PAD, channels), jnp.bfloat16)
    return pl.pallas_call(
        functools.partial(encode_kernel, order, len(arrived)),
        out_shape=[sent] * count,
        in_specs=vmem_specs(4 + len(arrived)),
        out_specs=vmem_specs(count),
        compiler_params=params(),
        cost_estimate=pl.CostEstimate(
            flops=2 * count * capacity * enc_weight.shape[0] * channels,
            bytes_accessed=2 * (3 * count * capacity + enc_weight.shape[0]) * channels,
            transcendentals=count * capacity * channels,
        ),
    )(enc_weight[None], g2m_coef, g2m_dst, picked, *arrived)


def gather_in_kernel(latent_ref, *refs):
    blocks, out_ref = (refs[:-1], refs[-1])
    nodes, channels = latent_ref.shape
    capacity = blocks[0].shape[0] - PAD
    rows16 = row_iota(nodes)
    pieces = capacity // channels
    total = latent_ref[...].astype(jnp.float32)
    for block in blocks:
        code = block[pl.ds(capacity, PAD), :].astype(jnp.float32)
        lines = [code[i : i + 1, :] for i in range(2 * pieces)]
        upper = lines[0] if pieces == 1 else jnp.concatenate(lines[:pieces], axis=1)
        lower = lines[1] if pieces == 1 else jnp.concatenate(lines[pieces:], axis=1)
        target = (8.0 * upper + lower).astype(jnp.int32)
        total += dot(sum_mask(target, rows16), block[pl.ds(0, capacity), :])
    out_ref[...] = total.astype(jnp.bfloat16)


def gather_in(mesh_latent, blocks):
    nodes, channels = mesh_latent.shape
    slots = len(blocks) * blocks[0].shape[0]
    return pl.pallas_call(
        gather_in_kernel,
        out_shape=jax.ShapeDtypeStruct((nodes, channels), jnp.bfloat16),
        in_specs=vmem_specs(1 + len(blocks)),
        out_specs=pl.BlockSpec(memory_space=pltpu.VMEM),
        compiler_params=params(),
        cost_estimate=pl.CostEstimate(
            flops=2 * nodes * slots * channels,
            bytes_accessed=2 * (slots + 2 * nodes) * channels,
            transcendentals=0,
        ),
    )(mesh_latent, *blocks)


def project_kernel(others, regions, offsets, src_ref, dst_ref, listed_ref, *refs):
    states, (sender_ref, receiver_ref, sent_ref) = (refs[: others + 1], refs[others + 1 :])
    nodes, channels = states[0].shape
    totals = []
    for weight_ref in (src_ref, dst_ref):
        weights = own_and_others_rows(weight_ref, channels, others)
        total = dot(states[0][...], weights[0])
        for state, weight in zip(states[1:], weights[1:]):
            total += dot(state[...], weight)
        totals.append(total.astype(jnp.bfloat16))
    sender_ref[...] = totals[0]
    receiver_ref[...] = totals[1]
    width = listed_ref.shape[2]
    lanes = lane_iota(nodes)
    region = lax.axis_index(REGION)
    sent_ref[...] = jnp.zeros_like(sent_ref)
    for j in range(0, len(offsets), 2):
        row = jnp.concatenate([listed_ref[0, pl.ds(j + i, 1), :] for i in range(2)], axis=1)
        rows = dot(pick_mask(column(row).astype(jnp.int16), lanes), totals[0]).astype(jnp.bfloat16)
        for i in range(2):
            to = region + offsets[j + i]

            @pl.when((to >= 0) & (to < regions))
            def _():
                sent_ref[jnp.clip(to, 0, regions - 1)] = rows[i * width : (i + 1) * width]


def project(layer, state, arrived, src_weights, dst_weights, halo_send, offsets):
    nodes, channels = state.shape
    links, width = halo_send.shape[1:]
    regions = lax.axis_size(REGION)
    depth = src_weights.shape[1]
    weight_spec = pl.BlockSpec((1, depth, channels), lambda i: (layer, 0, 0))
    table = jax.ShapeDtypeStruct((nodes, channels), jnp.bfloat16)
    return pl.pallas_call(
        functools.partial(project_kernel, len(arrived), regions, offsets),
        out_shape=[table, table, jax.ShapeDtypeStruct((regions, width, channels), jnp.bfloat16)],
        grid=(1,),
        in_specs=[weight_spec, weight_spec] + vmem_specs(2 + len(arrived)),
        out_specs=vmem_specs(3),
        compiler_params=params(),
        cost_estimate=pl.CostEstimate(
            flops=4 * nodes * depth * channels + 2 * links * width * nodes * channels,
            bytes_accessed=2 * (2 * depth + 4 * nodes + regions * width) * channels,
            transcendentals=0,
        ),
    )(src_weights, dst_weights, halo_send, state, *arrived)


def message_kernel(
    offsets, regions, turn, source_ref, target_ref, coef_ref, state_ref, sender_ref, receiver_ref, got_ref,
    out_ref, table_ref, total_ref,
):
    nodes, channels = state_ref.shape
    width = got_ref.shape[1]
    named = nodes + len(offsets) * width
    table_ref[pl.ds(0, nodes), :] = sender_ref[...]
    region = lax.axis_index(REGION)
    for j, offset in enumerate(offsets):
        origin = jnp.clip(region - offset, 0, regions - 1)
        table_ref[pl.ds(nodes + j * width, width), :] = got_ref[origin]
    table_ref[pl.ds(named, nodes), :] = receiver_ref[...]
    total_ref[...] = state_ref[...].astype(jnp.float32)
    source_lanes = lane_iota(named)
    target_lanes = lane_iota(nodes)
    rows16 = row_iota(nodes)

    def body(step, carry):
        start = pl.multiple_of(step * turn, turn)
        target = target_ref[:, pl.ds(start, turn)]
        source16 = column(source_ref[:, pl.ds(start, turn)]).astype(jnp.int16)
        target16 = column(target).astype(jnp.int16)
        mask = jnp.concatenate(
            [pick_mask(source16, source_lanes), pick_mask(target16, target_lanes)], axis=1
        )
        message = silu(dot(mask, table_ref[...])).astype(jnp.bfloat16)
        total_ref[...] += dot(sum_mask(target, rows16, coef_ref[:, pl.ds(start, turn)]), message)
        return carry

    lax.fori_loop(0, source_ref.shape[1] // turn, body, 0)
    out_ref[...] = total_ref[...].astype(jnp.bfloat16)


def messages(state, sender, receiver, got, m2m_src, m2m_dst, m2m_coef, offsets):
    nodes, channels = state.shape
    edges = m2m_src.shape[1]
    named = nodes + len(offsets) * got.shape[1]
    return pl.pallas_call(
        functools.partial(message_kernel, offsets, lax.axis_size(REGION), 512),
        out_shape=jax.ShapeDtypeStruct((nodes, channels), jnp.bfloat16),
        in_specs=vmem_specs(7),
        out_specs=pl.BlockSpec(memory_space=pltpu.VMEM),
        scratch_shapes=[
            pltpu.VMEM((named + nodes, channels), jnp.bfloat16),
            pltpu.VMEM((nodes, channels), jnp.float32),
        ],
        compiler_params=params(),
        cost_estimate=pl.CostEstimate(
            flops=2 * edges * (named + 2 * nodes) * channels,
            bytes_accessed=2 * (named + 3 * nodes) * channels,
            transcendentals=edges * channels,
        ),
    )(m2m_src, m2m_dst, m2m_coef, state, sender, receiver, got)


def on_device(
    grid_latent,
    enc_weight,
    mesh_latent,
    g2m_src,
    g2m_dst,
    g2m_coef,
    src_weights,
    dst_weights,
    halo_send,
    m2m_src,
    m2m_dst,
    m2m_coef,
):
    reach = (g2m_src.shape[1] - 1) // 2
    offsets = tuple(o for o in range(-reach, reach + 1) if o != 0)
    by_distance = sorted(range(2 * reach + 1), key=lambda j: -abs(j - reach))
    cut = len(by_distance) // 2 + 1
    groups = [tuple(by_distance[:cut]), tuple(by_distance[cut:])]
    blocks = []
    picked = [pick(order, g2m_src, grid_latent) for order in groups]
    arrived = [from_others(rows) for rows in picked]
    for order, rows, others in zip(groups, picked, arrived):
        encoded = encode(order, rows, others, enc_weight, g2m_coef, g2m_dst)
        for j, block in zip(order, encoded):
            blocks.append(block if j == reach else passed_along(block, j - reach))
    state = gather_in(mesh_latent, blocks)
    for layer in range(src_weights.shape[0]):
        sender, receiver, sent = project(
            layer, state, from_others(state), src_weights, dst_weights, halo_send, offsets
        )
        got = lax.all_to_all(sent, REGION, 0, 0, tiled=True)
        state = messages(state, sender, receiver, got, m2m_src, m2m_dst, m2m_coef, offsets)
    return state


def solution(mesh):
    placed = (
        P(("groups", "space", "edge"), "feat"),
        P(None, "feat"),
        P(("groups", "space", "edge"), "feat"),
        P(("groups", "space", "edge"), None, None),
        P(("groups", "space", "edge"), None, None),
        P(("groups", "space", "edge"), None, None),
        P(None, None, "feat"),
        P(None, None, "feat"),
        P(("groups", "space", "edge"), None, None),
        P(("groups", "space", "edge"), None),
        P(("groups", "space", "edge"), None),
        P(("groups", "space", "edge"), None),
    )
    return jax.shard_map(
        on_device,
        mesh=mesh,
        in_specs=placed,
        out_specs=P(("groups", "space", "edge"), "feat"),
        check_vma=False,
    )
```

```python
import functools

import jax
import jax.numpy as jnp
from jax import lax
from jax.experimental import pallas as pl
from jax.experimental.pallas import tpu as pltpu
from jax.sharding import PartitionSpec as P

REGION = ("space", "edge")
PAD = 16
VMEM_BYTES = 28 * 1024 * 1024


def made_in_vmem(output):
    return pltpu.VMEM(output.shape, output.dtype)


def taken_from_vmem(array):
    return pltpu.with_memory_space_constraint(array, pltpu.VMEM)


def call(kernel, outputs, inputs, flops, transcendentals=0, scratch=(), final=False):
    size = lambda a: int(a.size) * a.dtype.itemsize
    shapes = outputs if final else [made_in_vmem(o) for o in outputs]
    return pl.pallas_call(
        kernel,
        out_shape=shapes,
        in_specs=[pl.BlockSpec(memory_space=pltpu.VMEM)] * len(inputs),
        out_specs=[pl.BlockSpec(memory_space=pltpu.VMEM)] * len(outputs),
        scratch_shapes=list(scratch),
        compiler_params=pltpu.CompilerParams(vmem_limit_bytes=VMEM_BYTES),
        cost_estimate=pl.CostEstimate(
            flops=flops,
            bytes_accessed=sum(size(a) for a in list(inputs) + list(outputs)),
            transcendentals=transcendentals,
        ),
    )(*[taken_from_vmem(a) for a in inputs])


def shape(dims, dtype=jnp.bfloat16):
    return jax.ShapeDtypeStruct(dims, dtype)


def passed_along(value, steps):
    count = lax.axis_size(REGION)
    first, last = (max(0, -steps), min(count, count - steps))
    return lax.ppermute(value, REGION, [(i, i + steps) for i in range(first, last)])


def from_others(value):
    n = lax.axis_size("feat")
    return [
        lax.ppermute(value, "feat", [(i, (i + k) % n) for i in range(n)]) for k in range(1, n)
    ]


def own_and_others_rows(weight_ref, channels, others):
    n = others + 1
    me = lax.axis_index("feat")
    blocks = []
    for k in range(n):
        owner = lax.rem(me - k + n, n)
        start = pl.multiple_of(owner * channels, channels)
        blocks.append(weight_ref[pl.ds(start, channels), :])
    return blocks


def silu(v):
    half = 0.5 * v
    return half + half * jnp.tanh(half)


def column(row):
    length = row.shape[1]
    parts = [
        jnp.broadcast_to(row[:, c * 128 : (c + 1) * 128], (128, 128)).T for c in range(length // 128)
    ]
    return parts[0] if len(parts) == 1 else jnp.concatenate(parts, axis=0)


def lane_iota(count):
    return lax.broadcasted_iota(jnp.int32, (16, count), 1).astype(jnp.int16)


def row_iota(count):
    return lax.broadcasted_iota(jnp.int32, (count, 128), 0).astype(jnp.int16)


def tiled(value, rows, lanes):
    if value.shape[0] != rows:
        value = jnp.concatenate([value] * (rows // value.shape[0]), axis=0)
    if value.shape[1] != lanes:
        value = jnp.concatenate([value] * (lanes // value.shape[1]), axis=1)
    return value


def pick_mask(column16, lane16):
    rows, lanes = (column16.shape[0], lane16.shape[1])
    same = tiled(column16, rows, lanes) == tiled(lane16, rows, lanes)
    return jnp.where(same, jnp.bfloat16(1), jnp.bfloat16(0))


def sum_mask(row, rows16, scale=None):
    count, length = (rows16.shape[0], row.shape[1])
    targets = jnp.broadcast_to(row, (16, length)).astype(jnp.int16)
    same = tiled(rows16, count, length) == tiled(targets, count, length)
    if scale is None:
        here = jnp.bfloat16(1)
    else:
        here = tiled(jnp.broadcast_to(scale, (16, length)).astype(jnp.bfloat16), count, length)
    return jnp.where(same, here, jnp.bfloat16(0))


def dot(a, b):
    return jnp.dot(a, b, preferred_element_type=jnp.float32)


def pick_kernel(orders, index_ref, table_ref, *out_refs):
    lanes = lane_iota(table_ref.shape[0])
    for order, out_ref in zip(orders, out_refs):
        for place, j in enumerate(order):
            col = column(index_ref[j]).astype(jnp.int16)
            out_ref[place] = dot(pick_mask(col, lanes), table_ref[...]).astype(jnp.bfloat16)


def pick(orders, g2m_src, grid_latent):
    capacity = g2m_src.shape[2]
    rows, channels = grid_latent.shape
    return call(
        functools.partial(pick_kernel, orders),
        [shape((len(order), capacity, channels)) for order in orders],
        [g2m_src, grid_latent],
        2 * sum(map(len, orders)) * capacity * rows * channels,
    )


def encode_kernel(order, others, weight_ref, coef_ref, target_ref, *refs):
    sources, outs = (refs[: others + 1], refs[-len(order) :])
    capacity, channels = sources[0].shape[1:]
    weights = own_and_others_rows(weight_ref, channels, others)
    line = lax.broadcasted_iota(jnp.int32, (PAD, channels), 0)
    pieces = capacity // channels
    for place, j in enumerate(order):
        projected = dot(sources[0][place], weights[0])
        for source, weight in zip(sources[1:], weights[1:]):
            projected += dot(source[place], weight)
        scale = tiled(column(coef_ref[j]), capacity, channels)
        outs[place][pl.ds(0, capacity), :] = (scale * silu(projected)).astype(jnp.bfloat16)
        target = target_ref[j]
        code = jnp.zeros((PAD, channels), jnp.float32)
        for number, part in enumerate((target >> 3, target & 7)):
            part = part.astype(jnp.float32)
            for piece in range(pieces):
                values = part[:, piece * channels : (piece + 1) * channels]
                code = jnp.where(line == number * pieces + piece, values, code)
        outs[place][pl.ds(capacity, PAD), :] = code.astype(jnp.bfloat16)


def encode(order, picked, arrived, enc_weight, g2m_coef, g2m_dst, after=()):
    count, capacity, channels = picked.shape
    return call(
        functools.partial(encode_kernel, order, len(arrived)),
        [shape((capacity + PAD, channels))] * count,
        [enc_weight, g2m_coef, g2m_dst, picked, *arrived, *after],
        2 * count * capacity * enc_weight.shape[0] * channels,
        count * capacity * channels,
    )


def gather_in_kernel(before_ref, *refs):
    blocks, out_ref = (refs[:-1], refs[-1])
    nodes, channels = before_ref.shape
    capacity = blocks[0].shape[0] - PAD
    rows16 = row_iota(nodes)
    pieces = capacity // channels
    total = before_ref[...].astype(jnp.float32)
    for block in blocks:
        code = block[pl.ds(capacity, PAD), :].astype(jnp.float32)
        lines = [code[i : i + 1, :] for i in range(2 * pieces)]
        upper = lines[0] if pieces == 1 else jnp.concatenate(lines[:pieces], axis=1)
        lower = lines[1] if pieces == 1 else jnp.concatenate(lines[pieces:], axis=1)
        target = (8.0 * upper + lower).astype(jnp.int32)
        total += dot(sum_mask(target, rows16), block[pl.ds(0, capacity), :])
    out_ref[...] = total.astype(out_ref.dtype)


def gather_in(before, blocks, dtype):
    nodes, channels = before.shape
    slots = len(blocks) * blocks[0].shape[0]
    return call(
        gather_in_kernel,
        [shape((nodes, channels), dtype)],
        [before, *blocks],
        2 * nodes * slots * channels,
    )[0]


def columns_kernel(*refs):
    half = len(refs) // 2
    for row_ref, out_ref in zip(refs[:half], refs[half:]):
        out_ref[...] = column(row_ref[...]).astype(jnp.int16)


def columns(*rows):
    count = rows[0].shape[1]
    return call(
        columns_kernel, [shape((count, 128), jnp.int16)] * len(rows), rows, len(rows) * count * 128 * 8
    )


def project_kernel(
    others, reach, src_ref, dst_ref, listed_ref, *refs
):
    states, (sender_ref, receiver_ref, up_ref, down_ref, far_ref, near_ref) = (
        refs[: others + 1],
        refs[others + 1 :],
    )
    nodes, channels = states[0].shape
    for weight_ref, out_ref in ((src_ref, sender_ref), (dst_ref, receiver_ref)):
        weights = own_and_others_rows(weight_ref, channels, others)
        total = dot(states[0][...], weights[0])
        for state, weight in zip(states[1:], weights[1:]):
            total += dot(state[...], weight)
        out_ref[...] = total.astype(jnp.bfloat16)
    width = listed_ref.shape[2]
    lanes = lane_iota(nodes)
    core = lax.axis_index("edge")
    wanted = [2 - core, 3 - core, -2 - core, -1 - core, 6 * core - 3, 1 - 2 * core]
    wanted = [offset + reach - jnp.where(offset > 0, 1, 0) for offset in wanted]
    for k in range(0, len(wanted), 2):
        row = jnp.concatenate([listed_ref[wanted[k + i]] for i in range(2)], axis=1)
        rows = dot(pick_mask(column(row).astype(jnp.int16), lanes), sender_ref[...])
        rows = rows.astype(jnp.bfloat16)
        for i in range(2):
            part = rows[i * width : (i + 1) * width]
            if k == 0:
                up_ref[i] = part
            elif k == 2:
                down_ref[i] = part
            elif i == 0:
                far_ref[...] = part
            else:
                near_ref[...] = part


def project(state, arrived, src_weight, dst_weight, halo_send, reach):
    nodes, channels = state.shape
    links, unused, width = halo_send.shape
    depth = src_weight.shape[0]
    table, one, two = [shape(d) for d in ((nodes, channels), (width, channels), (2, width, channels))]
    return call(
        functools.partial(project_kernel, len(arrived), reach),
        [table, table, two, two, one, one],
        [src_weight, dst_weight, halo_send, state, *arrived],
        4 * nodes * depth * channels + 2 * links * width * nodes * channels,
    )


def forward_kernel(near_ref, from_below_ref, from_above_ref, out_ref):
    other = 1 - lax.axis_index("edge")
    out_ref[0] = near_ref[...]
    out_ref[1] = from_below_ref[other]
    out_ref[2] = from_above_ref[other]


def listed_rows(up, down, far, near):
    count = lax.axis_size(REGION)
    below = lax.ppermute(up, REGION, [(i, i + 2) for i in range(count - 2)])
    above = lax.ppermute(down, REGION, [(i, i - 2) for i in range(2, count)])
    odd = [(i, i + 3) for i in range(1, count - 3, 2)]
    even = [(i, i - 3) for i in range(4, count, 2)]
    distant = lax.ppermute(far, REGION, odd + even)
    width, channels = near.shape
    sent = call(forward_kernel, [shape((3, width, channels))], [near, below, above], 0)[0]
    across = lax.ppermute(sent, "edge", [(0, 1), (1, 0)])
    return below, above, distant, across


def first_kernel(turn, source_ref, target_ref, sender_ref, receiver_ref, out_ref):
    nodes = sender_ref.shape[0]
    lanes = lane_iota(nodes)
    for start in range(0, source_ref.shape[0], turn):
        here = pl.ds(start, turn)
        out_ref[here, :] = dot(pick_mask(source_ref[here, :], lanes), sender_ref[...]) + dot(
            pick_mask(target_ref[here, :], lanes), receiver_ref[...]
        )


def first_part(source_col, target_col, sender, receiver):
    nodes, channels = sender.shape
    edges = source_col.shape[0]
    return call(
        functools.partial(first_kernel, 512),
        [shape((edges, channels), jnp.float32)],
        [source_col, target_col, sender, receiver],
        4 * edges * nodes * channels,
    )[0]


def message_kernel(
    turn, source_ref, target_ref, coef_ref, state_ref, first_ref, below_ref, above_ref, distant_ref, across_ref,
    out_ref, table_ref,
):
    nodes, channels = state_ref.shape
    width = distant_ref.shape[0]
    core = lax.axis_index("edge")
    own_below, own_above = (below_ref[core], above_ref[core])
    even = core == 0
    rows = (
        jnp.where(even, across_ref[2], distant_ref[...]),
        own_above,
        jnp.where(even, across_ref[0], across_ref[2]),
        jnp.where(even, across_ref[1], across_ref[0]),
        own_below,
        jnp.where(even, distant_ref[...], across_ref[1]),
    )
    for j, part in enumerate(rows):
        table_ref[pl.ds(j * width, width), :] = part
    lanes = (lane_iota(len(rows) * width).astype(jnp.int32) + nodes).astype(jnp.int16)
    rows16 = row_iota(nodes)
    total = state_ref[...].astype(jnp.float32)
    for start in range(0, source_ref.shape[0], turn):
        here = pl.ds(start, turn)
        summed = first_ref[here, :] + dot(pick_mask(source_ref[here, :], lanes), table_ref[...])
        mask = sum_mask(target_ref[:, here], rows16, coef_ref[:, here])
        total += dot(mask, silu(summed).astype(jnp.bfloat16))
    out_ref[...] = total.astype(jnp.bfloat16)


def messages(source_col, m2m_dst, m2m_coef, state, first, listed, final):
    nodes, channels = state.shape
    edges = m2m_dst.shape[1]
    named = 6 * listed[2].shape[0]
    return call(
        functools.partial(message_kernel, 512),
        [shape((nodes, channels))],
        [source_col, m2m_dst, m2m_coef, state, first, *listed],
        2 * edges * (named + nodes) * channels,
        edges * channels,
        [pltpu.VMEM((named, channels), jnp.bfloat16)],
        final,
    )[0]


def on_device(
    grid_latent,
    enc_weight,
    mesh_latent,
    g2m_src,
    g2m_dst,
    g2m_coef,
    src_weights,
    dst_weights,
    halo_send,
    m2m_src,
    m2m_dst,
    m2m_coef,
):
    reach = (g2m_src.shape[1] - 1) // 2
    assert reach == 3 and lax.axis_size("edge") == 2
    g2m_src, g2m_dst, g2m_coef, halo_send = [
        jnp.swapaxes(a, 0, 1) for a in (g2m_src, g2m_dst, g2m_coef, halo_send)
    ]
    groups = [(reach - d, reach + d) for d in range(reach, 0, -1)] + [(reach,)]
    picked = pick(groups[:1], g2m_src, grid_latent) + pick(groups[1:], g2m_src, grid_latent)
    arrived = [from_others(rows) for rows in picked]
    source_col, target_col = columns(m2m_src, m2m_dst)
    blocks = []
    for order, rows, others in zip(groups, picked, arrived):
        after = () if blocks else (source_col, target_col)
        encoded = encode(order, rows, others, enc_weight, g2m_coef, g2m_dst, after)
        for j, block in zip(order, encoded):
            blocks.append(block if j == reach else passed_along(block, j - reach))
    state = gather_in(mesh_latent, blocks[:4], jnp.float32)
    state = gather_in(state, blocks[4:], jnp.bfloat16)
    layers = src_weights.shape[0]
    for layer in range(layers):
        sender, receiver, *sent = project(
            state, from_others(state), src_weights[layer], dst_weights[layer], halo_send, reach
        )
        listed = listed_rows(*sent)
        first = first_part(source_col, target_col, sender, receiver)
        state = messages(source_col, m2m_dst, m2m_coef, state, first, listed, layer == layers - 1)
    return state


def solution(mesh):
    placed = (
        P(("groups", "space", "edge"), "feat"),
        P(None, "feat"),
        P(("groups", "space", "edge"), "feat"),
        P(("groups", "space", "edge"), None, None),
        P(("groups", "space", "edge"), None, None),
        P(("groups", "space", "edge"), None, None),
        P(None, None, "feat"),
        P(None, None, "feat"),
        P(("groups", "space", "edge"), None, None),
        P(("groups", "space", "edge"), None),
        P(("groups", "space", "edge"), None),
        P(("groups", "space", "edge"), None),
    )
    return jax.shard_map(
        on_device,
        mesh=mesh,
        in_specs=placed,
        out_specs=P(("groups", "space", "edge"), "feat"),
        check_vma=False,
    )
```

```python
import functools

import jax
import jax.numpy as jnp
from jax import lax
from jax.experimental import pallas as pl
from jax.experimental.pallas import tpu as pltpu
from jax.sharding import PartitionSpec as P

REGION = ("space", "edge")
PAD = 16
VMEM_BYTES = 28 * 1024 * 1024


def made_in_vmem(output):
    return pltpu.VMEM(output.shape, output.dtype)


def taken_from_vmem(array):
    return pltpu.with_memory_space_constraint(array, pltpu.VMEM)


def call(kernel, outputs, inputs, flops, transcendentals=0, scratch=(), final=False, fetched=0):
    size = lambda a: int(a.size) * a.dtype.itemsize
    shapes = outputs if final else [made_in_vmem(o) for o in outputs]
    return pl.pallas_call(
        kernel,
        out_shape=shapes,
        in_specs=[pl.BlockSpec(memory_space=pltpu.VMEM)] * len(inputs),
        out_specs=[pl.BlockSpec(memory_space=pltpu.VMEM)] * len(outputs),
        scratch_shapes=list(scratch),
        compiler_params=pltpu.CompilerParams(vmem_limit_bytes=VMEM_BYTES),
        cost_estimate=pl.CostEstimate(
            flops=flops,
            bytes_accessed=sum(size(a) for a in list(inputs) + list(outputs)),
            transcendentals=transcendentals,
        ),
    )(*inputs[:fetched], *[taken_from_vmem(a) for a in inputs[fetched:]])


def shape(dims, dtype=jnp.bfloat16):
    return jax.ShapeDtypeStruct(dims, dtype)


def meets_core(r):
    return r + 1 - 2 * (r % 2)


def meets_next(r):
    return r - 1 + 2 * (r % 2)


def meets_two(r):
    return r + 2 - 4 * (r // 2 % 2)


def meets_other_two(r):
    return r - 2 + 4 * (r // 2 % 2)


def meets_three(r):
    return r + 3 - 6 * (r % 2)


def meets_other_three(r):
    return r - 3 + 6 * (r % 2)


def pairs(meets):
    count = lax.axis_size(REGION)
    return [(r, meets(r)) for r in range(count) if 0 <= meets(r) < count]


def swapped(value, meets):
    return lax.ppermute(value, REGION, pairs(meets))


def block_for(meets, reach):
    region = lax.axis_index(REGION)
    return meets(region) - region + reach


def from_others(value, meets=None):
    n = lax.axis_size("feat")
    if meets is None:
        axes, rings = ("feat", [[i for i in range(n)]])
    else:
        axes, cores = (("space", "feat", "edge"), lax.axis_size("edge"))
        rings = [
            [(r // cores * n + i) * cores + r % cores for i in range(n)] for r, unused in pairs(meets)
        ]
    return [
        lax.ppermute(value, axes, [(ring[i], ring[(i + k) % n]) for ring in rings for i in range(n)])
        for k in range(1, n)
    ]


def own_and_others_rows(weight_ref, channels, others):
    n = others + 1
    me = lax.axis_index("feat")
    blocks = []
    for k in range(n):
        owner = lax.rem(me - k + n, n)
        start = pl.multiple_of(owner * channels, channels)
        blocks.append(weight_ref[pl.ds(start, channels), :])
    return blocks


def silu(v):
    half = 0.5 * v
    return half + half * jnp.tanh(half)


def column(row):
    length = row.shape[1]
    parts = [
        jnp.broadcast_to(row[:, c * 128 : (c + 1) * 128], (128, 128)).T for c in range(length // 128)
    ]
    return parts[0] if len(parts) == 1 else jnp.concatenate(parts, axis=0)


def lane_iota(count):
    return lax.broadcasted_iota(jnp.int32, (16, count), 1).astype(jnp.int16)


def row_iota(count):
    return lax.broadcasted_iota(jnp.int32, (count, 128), 0).astype(jnp.int16)


def tiled(value, rows, lanes):
    if value.shape[0] != rows:
        value = jnp.concatenate([value] * (rows // value.shape[0]), axis=0)
    if value.shape[1] != lanes:
        value = jnp.concatenate([value] * (lanes // value.shape[1]), axis=1)
    return value


def pick_mask(column16, lane16):
    rows, lanes = (column16.shape[0], lane16.shape[1])
    same = tiled(column16, rows, lanes) == tiled(lane16, rows, lanes)
    return jnp.where(same, jnp.bfloat16(1), jnp.bfloat16(0))


def sum_mask(row, rows16, scale=None):
    count, length = (rows16.shape[0], row.shape[1])
    targets = jnp.broadcast_to(row, (16, length)).astype(jnp.int16)
    same = tiled(rows16, count, length) == tiled(targets, count, length)
    if scale is None:
        here = jnp.bfloat16(1)
    else:
        here = tiled(jnp.broadcast_to(scale, (16, length)).astype(jnp.bfloat16), count, length)
    return jnp.where(same, here, jnp.bfloat16(0))


def dot(a, b):
    return jnp.dot(a, b, preferred_element_type=jnp.float32)


def block_index(meets, reach):
    return reach if meets is None else block_for(meets, reach)


def pick_kernel(groups, index_ref, table_ref, *refs):
    out_refs = refs[-len(groups) :]
    lanes = lane_iota(table_ref.shape[0])
    reach = index_ref.shape[0] // 2
    for group, out_ref in zip(groups, out_refs):
        for place, meets in enumerate(group):
            col = column(index_ref[block_index(meets, reach)]).astype(jnp.int16)
            out_ref[place] = dot(pick_mask(col, lanes), table_ref[...]).astype(jnp.bfloat16)


def pick(groups, g2m_src, grid_latent, after=()):
    capacity = g2m_src.shape[2]
    rows, channels = grid_latent.shape
    return call(
        functools.partial(pick_kernel, groups),
        [shape((len(group), capacity, channels)) for group in groups],
        [g2m_src, grid_latent, *after],
        2 * sum(map(len, groups)) * capacity * rows * channels,
    )


def encode_kernel(group, others, weight_ref, coef_ref, target_ref, *refs):
    sources, outs = (refs[: others + 1], refs[-len(group) :])
    capacity, channels = sources[0].shape[1:]
    weights = own_and_others_rows(weight_ref, channels, others)
    line = lax.broadcasted_iota(jnp.int32, (PAD, channels), 0)
    pieces = capacity // channels
    reach = coef_ref.shape[0] // 2
    for place, meets in enumerate(group):
        j = block_index(meets, reach)
        projected = dot(sources[0][place], weights[0])
        for source, weight in zip(sources[1:], weights[1:]):
            projected += dot(source[place], weight)
        scale = tiled(column(coef_ref[j]), capacity, channels)
        outs[place][pl.ds(0, capacity), :] = (scale * silu(projected)).astype(jnp.bfloat16)
        target = target_ref[j]
        code = jnp.zeros((PAD, channels), jnp.float32)
        for number, part in enumerate((target >> 3, target & 7)):
            part = part.astype(jnp.float32)
            for piece in range(pieces):
                values = part[:, piece * channels : (piece + 1) * channels]
                code = jnp.where(line == number * pieces + piece, values, code)
        outs[place][pl.ds(capacity, PAD), :] = code.astype(jnp.bfloat16)


def encode(group, picked, arrived, enc_weight, g2m_coef, g2m_dst, after=()):
    count, capacity, channels = picked.shape
    return call(
        functools.partial(encode_kernel, group, len(arrived)),
        [shape((capacity + PAD, channels))] * count,
        [enc_weight, g2m_coef, g2m_dst, picked, *arrived, *after],
        2 * count * capacity * enc_weight.shape[0] * channels,
        count * capacity * channels,
    )


def gather_in_kernel(before_ref, *refs):
    blocks, out_ref = (refs[:-1], refs[-1])
    nodes, channels = before_ref.shape
    capacity = blocks[0].shape[0] - PAD
    rows16 = row_iota(nodes)
    pieces = capacity // channels
    total = before_ref[...].astype(jnp.float32)
    for block in blocks:
        code = block[pl.ds(capacity, PAD), :].astype(jnp.float32)
        lines = [code[i : i + 1, :] for i in range(2 * pieces)]
        upper = lines[0] if pieces == 1 else jnp.concatenate(lines[:pieces], axis=1)
        lower = lines[1] if pieces == 1 else jnp.concatenate(lines[pieces:], axis=1)
        target = (8.0 * upper + lower).astype(jnp.int32)
        total += dot(sum_mask(target, rows16), block[pl.ds(0, capacity), :])
    out_ref[...] = total.astype(out_ref.dtype)


def gather_in(before, blocks, dtype):
    nodes, channels = before.shape
    slots = len(blocks) * blocks[0].shape[0]
    return call(
        gather_in_kernel,
        [shape((nodes, channels), dtype)],
        [before, *blocks],
        2 * nodes * slots * channels,
    )[0]


def columns_kernel(pieces, *refs):
    rows = len(refs) // (pieces + 1)
    for k in range(rows):
        for piece, out_ref in enumerate(refs[rows + k * pieces : rows + (k + 1) * pieces]):
            count = out_ref.shape[0]
            out_ref[...] = column(refs[k][:, pl.ds(piece * count, count)]).astype(jnp.int16)


def columns(pieces, *rows):
    count = rows[0].shape[1] // pieces
    return call(
        functools.partial(columns_kernel, pieces),
        [shape((count, 128), jnp.int16)] * (pieces * len(rows)),
        rows,
        pieces * len(rows) * count * 128 * 8,
    )


def project_kernel(others, reach, src_ref, dst_ref, listed_ref, *refs):
    states, (sender_ref, receiver_ref, one_ref, two_ref, far_ref, near_ref) = (
        refs[: others + 1],
        refs[others + 1 :],
    )
    nodes, channels = states[0].shape
    for weight_ref, out_ref in ((src_ref, sender_ref), (dst_ref, receiver_ref)):
        weights = own_and_others_rows(weight_ref, channels, others)
        total = dot(states[0][...], weights[0])
        for state, weight in zip(states[1:], weights[1:]):
            total += dot(state[...], weight)
        out_ref[...] = total.astype(jnp.bfloat16)
    width = listed_ref.shape[2]
    lanes = lane_iota(nodes)
    region = lax.axis_index(REGION)
    core = region % 2
    wanted = [
        meets(region) - core + i - region for meets in (meets_two, meets_other_two) for i in range(2)
    ]
    wanted += [meets_other_three(region) - region, meets_core(region) - region]
    wanted = [offset + reach - jnp.where(offset > 0, 1, 0) for offset in wanted]
    for k in range(0, len(wanted), 2):
        row = jnp.concatenate([listed_ref[wanted[k + i]] for i in range(2)], axis=1)
        rows = dot(pick_mask(column(row).astype(jnp.int16), lanes), sender_ref[...])
        rows = rows.astype(jnp.bfloat16)
        parts = [rows[i * width : (i + 1) * width] for i in range(2)]
        if k < 4:
            ref = one_ref if k == 0 else two_ref
            for i in range(2):
                ref[i] = parts[i]
        else:
            far_ref[...] = parts[0]
            near_ref[...] = parts[1]


def project(state, arrived, src_weight, dst_weight, halo_send, reach):
    nodes, channels = state.shape
    links, unused, width = halo_send.shape
    depth = src_weight.shape[0]
    table, one, two = [shape(d) for d in ((nodes, channels), (width, channels), (2, width, channels))]
    return call(
        functools.partial(project_kernel, len(arrived), reach),
        [table, table, two, two, one, one],
        [src_weight, dst_weight, halo_send, state, *arrived],
        4 * nodes * depth * channels + 2 * links * width * nodes * channels,
    )


def forward_kernel(near_ref, one_ref, two_ref, unused_ref, out_ref):
    other = 1 - lax.axis_index("edge")
    out_ref[0] = near_ref[...]
    out_ref[1] = one_ref[other]
    out_ref[2] = two_ref[other]


def first_kernel(turn, source_ref, target_ref, sender_ref, receiver_ref, *refs):
    out_ref = refs[-1]
    nodes = sender_ref.shape[0]
    lanes = lane_iota(nodes)
    for start in range(0, source_ref.shape[0], turn):
        here = pl.ds(start, turn)
        out_ref[here, :] = dot(pick_mask(source_ref[here, :], lanes), sender_ref[...]) + dot(
            pick_mask(target_ref[here, :], lanes), receiver_ref[...]
        )


def first_part(source_col, target_col, sender, receiver, after=()):
    nodes, channels = sender.shape
    edges = source_col.shape[0]
    return call(
        functools.partial(first_kernel, 512),
        [shape((edges, channels), jnp.float32)],
        [source_col, target_col, sender, receiver, *after],
        4 * edges * nodes * channels,
    )[0]


def message_kernel(
    turn, halves, target_ref, coef_ref, state_ref, one_ref, two_ref, distant_ref, across_ref, *refs
):
    sources, firsts, (out_ref, table_ref) = (refs[:halves], refs[halves : 2 * halves], refs[2 * halves :])
    nodes, channels = state_ref.shape
    width = distant_ref.shape[0]
    region = lax.axis_index(REGION)
    core = region % 2
    low_even = region // 2 % 2 == 0
    own = (one_ref[core], two_ref[core])
    across = (across_ref[1], across_ref[2])
    before, after = [
        [jnp.where(low_even == first, pair[0], pair[1]) for pair in (own, across)] for first in (False, True)
    ]
    near = across_ref[0]
    distant = distant_ref[...]
    even = core == 0
    rows = (
        jnp.where(even, after[1], distant),
        after[0],
        jnp.where(even, near, after[1]),
        jnp.where(even, before[1], near),
        before[0],
        jnp.where(even, distant, before[1]),
    )
    for j, part in enumerate(rows):
        table_ref[pl.ds(j * width, width), :] = part
    lanes = (lane_iota(len(rows) * width).astype(jnp.int32) + nodes).astype(jnp.int16)
    rows16 = row_iota(nodes)
    total = state_ref[...].astype(jnp.float32)
    for half, (source_ref, first_ref) in enumerate(zip(sources, firsts)):
        count = source_ref.shape[0]
        for start in range(0, count, turn):
            here = pl.ds(start, turn)
            there = pl.ds(half * count + start, turn)
            summed = first_ref[here, :] + dot(pick_mask(source_ref[here, :], lanes), table_ref[...])
            mask = sum_mask(target_ref[:, there], rows16, coef_ref[:, there])
            total += dot(mask, silu(summed).astype(jnp.bfloat16))
    out_ref[...] = total.astype(jnp.bfloat16)


def messages(m2m_dst, m2m_coef, state, listed, sources, firsts, final):
    nodes, channels = state.shape
    edges = m2m_dst.shape[1]
    named = 6 * listed[2].shape[0]
    return call(
        functools.partial(message_kernel, 512, len(sources)),
        [shape((nodes, channels))],
        [m2m_dst, m2m_coef, state, *listed, *sources, *firsts],
        2 * edges * (named + nodes) * channels,
        edges * channels,
        [pltpu.VMEM((named, channels), jnp.bfloat16)],
        final,
    )[0]


def on_device(
    grid_latent,
    enc_weight,
    mesh_latent,
    g2m_src,
    g2m_dst,
    g2m_coef,
    src_weights,
    dst_weights,
    halo_send,
    m2m_src,
    m2m_dst,
    m2m_coef,
):
    reach = (g2m_src.shape[1] - 1) // 2
    assert reach == 3 and lax.axis_size("edge") == 2
    g2m_src, g2m_dst, g2m_coef, halo_send = [
        jnp.swapaxes(a, 0, 1) for a in (g2m_src, g2m_dst, g2m_coef, halo_send)
    ]
    cols = columns(2, m2m_src, m2m_dst)
    source_cols, target_cols = cols[:2], cols[2:]
    groups = [(meets_three,), (meets_other_three,), (meets_two, meets_other_two, meets_next), (meets_core, None)]
    picked = pick(groups[:2], g2m_src, grid_latent)
    arrived = [from_others(rows, group[0]) for group, rows in zip(groups, picked)]
    for place in (2, 3):
        picked += pick(groups[place : place + 1], g2m_src, grid_latent, arrived[place - 2])
        arrived.append(from_others(picked[place]))
    state = mesh_latent
    after = cols
    waiting = []
    for place, (group, rows, others) in enumerate(zip(groups, picked, arrived)):
        encoded = encode(group, rows, others, enc_weight, g2m_coef, g2m_dst, after)
        waiting += [
            block if meets is None else swapped(block, meets) for meets, block in zip(group, encoded)
        ]
        if place == 1:
            state = gather_in(state, waiting, jnp.float32)
            waiting, after = ([], [state])
    state = gather_in(state, waiting[:2], jnp.float32)
    state = gather_in(state, waiting[2:], jnp.bfloat16)
    layers = src_weights.shape[0]
    for layer in range(layers):
        sender, receiver, one, two, far, near = project(
            state, from_others(state), src_weights[layer], dst_weights[layer], halo_send, reach
        )
        one, two = swapped(one, meets_two), swapped(two, meets_other_two)
        distant = swapped(far, meets_other_three)
        firsts = [first_part(source_cols[0], target_cols[0], sender, receiver)]
        width, channels = near.shape
        sent = call(
            forward_kernel, [shape((3, width, channels))], [near, one, two, firsts[0]], 3 * width * channels
        )[0]
        across = swapped(sent, meets_core)
        firsts.append(first_part(source_cols[1], target_cols[1], sender, receiver, [sent]))
        state = messages(
            m2m_dst, m2m_coef, state, (one, two, distant, across), source_cols, firsts, layer == layers - 1
        )
    return state


def solution(mesh):
    placed = (
        P(("groups", "space", "edge"), "feat"),
        P(None, "feat"),
        P(("groups", "space", "edge"), "feat"),
        P(("groups", "space", "edge"), None, None),
        P(("groups", "space", "edge"), None, None),
        P(("groups", "space", "edge"), None, None),
        P(None, None, "feat"),
        P(None, None, "feat"),
        P(("groups", "space", "edge"), None, None),
        P(("groups", "space", "edge"), None),
        P(("groups", "space", "edge"), None),
        P(("groups", "space", "edge"), None),
    )
    return jax.shard_map(
        on_device,
        mesh=mesh,
        in_specs=placed,
        out_specs=P(("groups", "space", "edge"), "feat"),
        check_vma=False,
    )
```

```python
import functools

import jax
import jax.numpy as jnp
from jax import lax
from jax.experimental import pallas as pl
from jax.experimental.pallas import tpu as pltpu
from jax.sharding import PartitionSpec as P

REGION = ("space", "edge")
PAD = 16
VMEM_BYTES = 28 * 1024 * 1024


def made_in_vmem(output):
    return pltpu.VMEM(output.shape, output.dtype)


def taken_from_vmem(array):
    return pltpu.with_memory_space_constraint(array, pltpu.VMEM)


def call(kernel, outputs, inputs, flops, transcendentals=0, scratch=(), final=False, fetched=0):
    size = lambda a: int(a.size) * a.dtype.itemsize
    shapes = outputs if final else [made_in_vmem(o) for o in outputs]
    return pl.pallas_call(
        kernel,
        out_shape=shapes,
        in_specs=[pl.BlockSpec(memory_space=pltpu.VMEM)] * len(inputs),
        out_specs=[pl.BlockSpec(memory_space=pltpu.VMEM)] * len(outputs),
        scratch_shapes=list(scratch),
        compiler_params=pltpu.CompilerParams(vmem_limit_bytes=VMEM_BYTES),
        cost_estimate=pl.CostEstimate(
            flops=flops,
            bytes_accessed=sum(size(a) for a in list(inputs) + list(outputs)) if flops else 0,
            transcendentals=transcendentals,
        ),
    )(*inputs[:fetched], *[taken_from_vmem(a) for a in inputs[fetched:]])


def shape(dims, dtype=jnp.bfloat16):
    return jax.ShapeDtypeStruct(dims, dtype)


def meets_core(r):
    return r + 1 - 2 * (r % 2)


def meets_next(r):
    return r - 1 + 2 * (r % 2)


def meets_two(r):
    return r + 2 - 4 * (r // 2 % 2)


def meets_other_two(r):
    return r - 2 + 4 * (r // 2 % 2)


def meets_three(r):
    return r + 3 - 6 * (r % 2)


def meets_other_three(r):
    return r - 3 + 6 * (r % 2)


def pairs(meets):
    count = lax.axis_size(REGION)
    return [(r, meets(r)) for r in range(count) if 0 <= meets(r) < count]


def swapped(value, meets):
    return lax.ppermute(value, REGION, pairs(meets))


def block_for(meets, reach):
    region = lax.axis_index(REGION)
    return meets(region) - region + reach


def from_others(value, meets=None):
    n = lax.axis_size("feat")
    if meets is None:
        axes, rings = ("feat", [[i for i in range(n)]])
    else:
        axes, cores = (("space", "feat", "edge"), lax.axis_size("edge"))
        rings = [
            [(r // cores * n + i) * cores + r % cores for i in range(n)] for r, unused in pairs(meets)
        ]
    return [
        lax.ppermute(value, axes, [(ring[i], ring[(i + k) % n]) for ring in rings for i in range(n)])
        for k in range(1, n)
    ]


def own_and_others_rows(weight_ref, channels, others):
    n = others + 1
    me = lax.axis_index("feat")
    blocks = []
    for k in range(n):
        owner = lax.rem(me - k + n, n)
        start = pl.multiple_of(owner * channels, channels)
        blocks.append(weight_ref[pl.ds(start, channels), :])
    return blocks


def silu(v):
    half = 0.5 * v
    return half + half * jnp.tanh(half)


def column(row):
    length = row.shape[1]
    parts = [
        jnp.broadcast_to(row[:, c * 128 : (c + 1) * 128], (128, 128)).T for c in range(length // 128)
    ]
    return parts[0] if len(parts) == 1 else jnp.concatenate(parts, axis=0)


def lane_iota(count):
    return lax.broadcasted_iota(jnp.int32, (16, count), 1).astype(jnp.int16)


def row_iota(count):
    return lax.broadcasted_iota(jnp.int32, (count, 128), 0).astype(jnp.int16)


def tiled(value, rows, lanes):
    if value.shape[0] != rows:
        value = jnp.concatenate([value] * (rows // value.shape[0]), axis=0)
    if value.shape[1] != lanes:
        value = jnp.concatenate([value] * (lanes // value.shape[1]), axis=1)
    return value


def pick_mask(column16, lane16):
    rows, lanes = (column16.shape[0], lane16.shape[1])
    same = tiled(column16, rows, lanes) == tiled(lane16, rows, lanes)
    return jnp.where(same, jnp.bfloat16(1), jnp.bfloat16(0))


def sum_mask(row, rows16, scale=None):
    count, length = (rows16.shape[0], row.shape[1])
    targets = jnp.broadcast_to(row, (16, length)).astype(jnp.int16)
    same = tiled(rows16, count, length) == tiled(targets, count, length)
    if scale is None:
        here = jnp.bfloat16(1)
    else:
        here = tiled(jnp.broadcast_to(scale, (16, length)).astype(jnp.bfloat16), count, length)
    return jnp.where(same, here, jnp.bfloat16(0))


def dot(a, b):
    return jnp.dot(a, b, preferred_element_type=jnp.float32)


def block_index(meets, reach):
    return reach if meets is None else block_for(meets, reach)


def pick_kernel(groups, index_ref, table_ref, *refs):
    out_refs = refs[-len(groups) :]
    lanes = lane_iota(table_ref.shape[0])
    reach = index_ref.shape[0] // 2
    for group, out_ref in zip(groups, out_refs):
        for place, meets in enumerate(group):
            col = column(index_ref[block_index(meets, reach)]).astype(jnp.int16)
            out_ref[place] = dot(pick_mask(col, lanes), table_ref[...]).astype(jnp.bfloat16)


def pick(groups, g2m_src, grid_latent, after=()):
    capacity = g2m_src.shape[2]
    rows, channels = grid_latent.shape
    return call(
        functools.partial(pick_kernel, groups),
        [shape((len(group), capacity, channels)) for group in groups],
        [g2m_src, grid_latent, *after],
        2 * sum(map(len, groups)) * capacity * rows * channels,
    )


def encode_kernel(group, others, weight_ref, coef_ref, target_ref, *refs):
    sources, outs = (refs[: others + 1], refs[-len(group) :])
    capacity, channels = sources[0].shape[1:]
    weights = own_and_others_rows(weight_ref, channels, others)
    line = lax.broadcasted_iota(jnp.int32, (PAD, channels), 0)
    pieces = capacity // channels
    reach = coef_ref.shape[0] // 2
    for place, meets in enumerate(group):
        j = block_index(meets, reach)
        projected = dot(sources[0][place], weights[0])
        for source, weight in zip(sources[1:], weights[1:]):
            projected += dot(source[place], weight)
        scale = tiled(column(coef_ref[j]), capacity, channels)
        outs[place][pl.ds(0, capacity), :] = (scale * silu(projected)).astype(jnp.bfloat16)
        target = target_ref[j]
        code = jnp.zeros((PAD, channels), jnp.float32)
        for number, part in enumerate((target >> 3, target & 7)):
            part = part.astype(jnp.float32)
            for piece in range(pieces):
                values = part[:, piece * channels : (piece + 1) * channels]
                code = jnp.where(line == number * pieces + piece, values, code)
        outs[place][pl.ds(capacity, PAD), :] = code.astype(jnp.bfloat16)


def encode(group, picked, arrived, enc_weight, g2m_coef, g2m_dst, after=()):
    count, capacity, channels = picked.shape
    return call(
        functools.partial(encode_kernel, group, len(arrived)),
        [shape((capacity + PAD, channels))] * count,
        [enc_weight, g2m_coef, g2m_dst, picked, *arrived, *after],
        2 * count * capacity * enc_weight.shape[0] * channels,
        count * capacity * channels,
    )


def gather_in_kernel(before_ref, *refs):
    blocks, out_ref = (refs[:-1], refs[-1])
    nodes, channels = before_ref.shape
    capacity = blocks[0].shape[0] - PAD
    rows16 = row_iota(nodes)
    pieces = capacity // channels
    total = before_ref[...].astype(jnp.float32)
    for block in blocks:
        code = block[pl.ds(capacity, PAD), :].astype(jnp.float32)
        lines = [code[i : i + 1, :] for i in range(2 * pieces)]
        upper = lines[0] if pieces == 1 else jnp.concatenate(lines[:pieces], axis=1)
        lower = lines[1] if pieces == 1 else jnp.concatenate(lines[pieces:], axis=1)
        target = (8.0 * upper + lower).astype(jnp.int32)
        total += dot(sum_mask(target, rows16), block[pl.ds(0, capacity), :])
    out_ref[...] = total.astype(out_ref.dtype)


def gather_in(before, blocks, dtype):
    nodes, channels = before.shape
    slots = len(blocks) * blocks[0].shape[0]
    return call(
        gather_in_kernel,
        [shape((nodes, channels), dtype)],
        [before, *blocks],
        2 * nodes * slots * channels,
    )[0]


def columns_kernel(pieces, *refs):
    rows = len(refs) // (pieces + 1)
    for k in range(rows):
        for piece, out_ref in enumerate(refs[rows + k * pieces : rows + (k + 1) * pieces]):
            count = out_ref.shape[0]
            out_ref[...] = column(refs[k][:, pl.ds(piece * count, count)]).astype(jnp.int16)


def columns(pieces, *rows):
    count = rows[0].shape[1] // pieces
    return call(
        functools.partial(columns_kernel, pieces),
        [shape((count, 128), jnp.int16)] * (pieces * len(rows)),
        rows,
        pieces * len(rows) * count * 128 * 8,
    )


def list_kernel(reach, listed_ref, state_ref, one_ref, two_ref, far_ref, near_ref):
    nodes = state_ref.shape[0]
    width = listed_ref.shape[2]
    lanes = lane_iota(nodes)
    region = lax.axis_index(REGION)
    core = region % 2
    wanted = [
        meets(region) - core + i - region for meets in (meets_two, meets_other_two) for i in range(2)
    ]
    wanted += [meets_other_three(region) - region, meets_core(region) - region]
    wanted = [offset + reach - jnp.where(offset > 0, 1, 0) for offset in wanted]
    for k in range(0, len(wanted), 2):
        row = jnp.concatenate([listed_ref[wanted[k + i]] for i in range(2)], axis=1)
        rows = dot(pick_mask(column(row).astype(jnp.int16), lanes), state_ref[...])
        rows = rows.astype(jnp.bfloat16)
        parts = [rows[i * width : (i + 1) * width] for i in range(2)]
        if k < 4:
            ref = one_ref if k == 0 else two_ref
            for i in range(2):
                ref[i] = parts[i]
        else:
            far_ref[...] = parts[0]
            near_ref[...] = parts[1]


def list_rows(state, halo_send, reach):
    nodes, channels = state.shape
    links, unused, width = halo_send.shape
    one, two = [shape(d) for d in ((width, channels), (2, width, channels))]
    return call(
        functools.partial(list_kernel, reach),
        [two, two, one, one],
        [halo_send, state],
        0,
    )


def forward_kernel(near_ref, one_ref, two_ref, out_ref):
    other = 1 - lax.axis_index("edge")
    out_ref[0] = near_ref[...]
    out_ref[1] = one_ref[other]
    out_ref[2] = two_ref[other]


def order_kernel(one_ref, two_ref, distant_ref, across_ref, out_ref):
    width = distant_ref.shape[0]
    region = lax.axis_index(REGION)
    core = region % 2
    low_even = region // 2 % 2 == 0
    own = (one_ref[core], two_ref[core])
    across = (across_ref[1], across_ref[2])
    before, after = [
        [jnp.where(low_even == first, pair[0], pair[1]) for pair in (own, across)] for first in (False, True)
    ]
    near = across_ref[0]
    distant = distant_ref[...]
    even = core == 0
    rows = (
        jnp.where(even, after[1], distant),
        after[0],
        jnp.where(even, near, after[1]),
        jnp.where(even, before[1], near),
        before[0],
        jnp.where(even, distant, before[1]),
    )
    for j, part in enumerate(rows):
        out_ref[pl.ds(j * width, width), :] = part


def exchange_listed(one, two, far, near):
    width, channels = near.shape
    one, two = swapped(one, meets_two), swapped(two, meets_other_two)
    distant = swapped(far, meets_other_three)
    sent = call(forward_kernel, [shape((3, width, channels))], [near, one, two], 0)[0]
    across = swapped(sent, meets_core)
    return call(
        order_kernel, [shape((6 * width, channels))], [one, two, distant, across], 0
    )[0]


def projected_rows(weight_ref, parts):
    weights = own_and_others_rows(weight_ref, parts[0].shape[1], len(parts) - 1)
    total = dot(parts[0][...], weights[0])
    for part, weight in zip(parts[1:], weights[1:]):
        total += dot(part[...], weight)
    return total.astype(jnp.bfloat16)


def project_kernel(src_ref, dst_ref, *refs):
    states, table_ref = (refs[:-1], refs[-1])
    nodes = states[0].shape[0]
    table_ref[pl.ds(0, nodes), :] = projected_rows(src_ref, states)
    table_ref[pl.ds(nodes, nodes), :] = projected_rows(dst_ref, states)


def project(states, src_weight, dst_weight):
    nodes, channels = states[0].shape
    depth = src_weight.shape[0]
    return call(
        project_kernel,
        [shape((2 * nodes, channels))],
        [src_weight, dst_weight, *states],
        4 * nodes * depth * channels,
    )[0]


def first_kernel(turn, source_ref, target_ref, table_ref, out_ref):
    lanes = lane_iota(table_ref.shape[0] // 2)
    for start in range(0, source_ref.shape[0], turn):
        here = pl.ds(start, turn)
        mask = jnp.concatenate(
            [pick_mask(source_ref[here, :], lanes), pick_mask(target_ref[here, :], lanes)], axis=1
        )
        out_ref[here, :] = dot(mask, table_ref[...])


def first_part(source_col, target_col, table):
    rows, channels = table.shape
    edges = source_col.shape[0]
    return call(
        functools.partial(first_kernel, 512),
        [shape((edges, channels), jnp.float32)],
        [source_col, target_col, table],
        2 * edges * rows * channels,
    )[0]


def message_kernel(turn, source_ref, target_ref, coef_ref, state_ref, first_ref, weight_ref, *refs):
    listed, (out_ref, message_ref) = (refs[:-2], refs[-2:])
    nodes, channels = state_ref.shape
    table = projected_rows(weight_ref, listed)
    lanes = (lane_iota(table.shape[0]).astype(jnp.int32) + nodes).astype(jnp.int16)
    rows16 = row_iota(nodes)
    total = state_ref[...].astype(jnp.float32)
    for start in range(0, source_ref.shape[0], turn):
        here = pl.ds(start, turn)
        summed = first_ref[here, :] + dot(pick_mask(source_ref[here, :], lanes), table)
        message_ref[here, :] = silu(summed).astype(jnp.bfloat16)
        mask = sum_mask(target_ref[:, here], rows16, coef_ref[:, here])
        total += dot(mask, message_ref[here, :])
    out_ref[...] = total.astype(jnp.bfloat16)


def messages(source_col, m2m_dst, m2m_coef, state, first, src_weight, listed, final):
    nodes, channels = state.shape
    edges = m2m_dst.shape[1]
    named = listed[0].shape[0]
    return call(
        functools.partial(message_kernel, 1024),
        [shape((nodes, channels))],
        [source_col, m2m_dst, m2m_coef, state, first, src_weight, *listed],
        2 * edges * (named + nodes) * channels,
        edges * channels,
        [pltpu.VMEM((edges, channels), jnp.bfloat16)],
        final,
    )[0]


def on_device(
    grid_latent,
    enc_weight,
    mesh_latent,
    g2m_src,
    g2m_dst,
    g2m_coef,
    src_weights,
    dst_weights,
    halo_send,
    m2m_src,
    m2m_dst,
    m2m_coef,
):
    reach = (g2m_src.shape[1] - 1) // 2
    assert reach == 3 and lax.axis_size("edge") == 2
    g2m_src, g2m_dst, g2m_coef, halo_send = [
        jnp.swapaxes(a, 0, 1) for a in (g2m_src, g2m_dst, g2m_coef, halo_send)
    ]
    source_col, target_col = cols = columns(1, m2m_src, m2m_dst)
    groups = [
        (meets_three,), (meets_other_three,), (meets_two, meets_other_two), (meets_next,), (meets_core, None)
    ]
    picked = pick(groups[:2], g2m_src, grid_latent)
    arrived = [from_others(rows, group[0]) for group, rows in zip(groups, picked)]
    for place, before in ((2, 0), (3, 1), (4, 3)):
        picked += pick(groups[place : place + 1], g2m_src, grid_latent, arrived[before])
        arrived.append(from_others(picked[place]))
    sent = []
    state = mesh_latent
    for place in (0, 1, 3, 2, 4):
        after = {0: cols, 2: [state]}.get(place, ())
        encoded = encode(groups[place], picked[place], arrived[place], enc_weight, g2m_coef, g2m_dst, after)
        sent += [
            block if meets is None else swapped(block, meets) for meets, block in zip(groups[place], encoded)
        ]
        if place == 3:
            state = gather_in(state, sent[:2], jnp.float32)
    state = gather_in(state, sent[2:5], jnp.float32)
    state = gather_in(state, sent[5:], jnp.bfloat16)
    layers = src_weights.shape[0]
    for layer in range(layers):
        src_weight, dst_weight = src_weights[layer], dst_weights[layer]
        others = from_others(state)
        listed = exchange_listed(*list_rows(state, halo_send, reach))
        table = project([state, *others], src_weight, dst_weight)
        listed = [listed, *from_others(listed)]
        first = first_part(source_col, target_col, table)
        state = messages(
            source_col, m2m_dst, m2m_coef, state, first, src_weight, listed, layer == layers - 1
        )
    return state


def solution(mesh):
    placed = (
        P(("groups", "space", "edge"), "feat"),
        P(None, "feat"),
        P(("groups", "space", "edge"), "feat"),
        P(("groups", "space", "edge"), None, None),
        P(("groups", "space", "edge"), None, None),
        P(("groups", "space", "edge"), None, None),
        P(None, None, "feat"),
        P(None, None, "feat"),
        P(("groups", "space", "edge"), None, None),
        P(("groups", "space", "edge"), None),
        P(("groups", "space", "edge"), None),
        P(("groups", "space", "edge"), None),
    )
    return jax.shard_map(
        on_device,
        mesh=mesh,
        in_specs=placed,
        out_specs=P(("groups", "space", "edge"), "feat"),
        check_vma=False,
    )
```

```python
import functools

import jax
import jax.numpy as jnp
from jax import lax
from jax.experimental import pallas as pl
from jax.experimental.pallas import tpu as pltpu
from jax.sharding import PartitionSpec as P

REGION = ("space", "edge")
PAD = 16
VMEM_BYTES = 28 * 1024 * 1024


def made_in_vmem(output):
    return pltpu.VMEM(output.shape, output.dtype)


def taken_from_vmem(array):
    return pltpu.with_memory_space_constraint(array, pltpu.VMEM)


def taken_from_hbm(array):
    return pltpu.with_memory_space_constraint(array, pltpu.HBM)


def call(kernel, outputs, inputs, flops, transcendentals=0, scratch=(), final=False, fetched=0):
    size = lambda a: int(a.size) * a.dtype.itemsize
    shapes = outputs if final else [made_in_vmem(o) for o in outputs]
    return pl.pallas_call(
        kernel,
        out_shape=shapes,
        in_specs=[pl.BlockSpec(memory_space=pltpu.VMEM)] * len(inputs),
        out_specs=[pl.BlockSpec(memory_space=pltpu.VMEM)] * len(outputs),
        scratch_shapes=list(scratch),
        compiler_params=pltpu.CompilerParams(vmem_limit_bytes=VMEM_BYTES),
        cost_estimate=pl.CostEstimate(
            flops=flops,
            bytes_accessed=sum(size(a) for a in list(inputs) + list(outputs)) if flops else 0,
            transcendentals=transcendentals,
        ),
    )(*inputs[:fetched], *[taken_from_vmem(a) for a in inputs[fetched:]])


def shape(dims, dtype=jnp.bfloat16):
    return jax.ShapeDtypeStruct(dims, dtype)


def meets_core(r):
    return r + 1 - 2 * (r % 2)


def meets_next(r):
    return r - 1 + 2 * (r % 2)


def meets_two(r):
    return r + 2 - 4 * (r // 2 % 2)


def meets_other_two(r):
    return r - 2 + 4 * (r // 2 % 2)


def meets_three(r):
    return r + 3 - 6 * (r % 2)


def meets_other_three(r):
    return r - 3 + 6 * (r % 2)


def pairs(meets):
    count = lax.axis_size(REGION)
    return [(r, meets(r)) for r in range(count) if 0 <= meets(r) < count]


def swapped(value, meets):
    return lax.ppermute(value, REGION, pairs(meets))


def block_for(meets, reach):
    region = lax.axis_index(REGION)
    return meets(region) - region + reach


def from_others(value, meets=None):
    n = lax.axis_size("feat")
    if meets is None:
        axes, rings = ("feat", [[i for i in range(n)]])
    else:
        axes, cores = (("space", "feat", "edge"), lax.axis_size("edge"))
        rings = [
            [(r // cores * n + i) * cores + r % cores for i in range(n)] for r, unused in pairs(meets)
        ]
    return [
        lax.ppermute(value, axes, [(ring[i], ring[(i + k) % n]) for ring in rings for i in range(n)])
        for k in range(1, n)
    ]


def own_and_others_rows(weight_ref, channels, others):
    n = others + 1
    me = lax.axis_index("feat")
    blocks = []
    for k in range(n):
        owner = lax.rem(me - k + n, n)
        start = pl.multiple_of(owner * channels, channels)
        blocks.append(weight_ref[pl.ds(start, channels), :])
    return blocks


def silu(v):
    half = 0.5 * v
    return half + half * jnp.tanh(half)


def column(row):
    length = row.shape[1]
    parts = [
        jnp.broadcast_to(row[:, c * 128 : (c + 1) * 128], (128, 128)).T for c in range(length // 128)
    ]
    return parts[0] if len(parts) == 1 else jnp.concatenate(parts, axis=0)


def lane_iota(count):
    return lax.broadcasted_iota(jnp.int32, (16, count), 1).astype(jnp.int16)


def row_iota(count):
    return lax.broadcasted_iota(jnp.int32, (count, 128), 0).astype(jnp.int16)


def tiled(value, rows, lanes):
    if value.shape[0] != rows:
        value = jnp.concatenate([value] * (rows // value.shape[0]), axis=0)
    if value.shape[1] != lanes:
        value = jnp.concatenate([value] * (lanes // value.shape[1]), axis=1)
    return value


def pick_mask(column16, lane16):
    rows, lanes = (column16.shape[0], lane16.shape[1])
    same = tiled(column16, rows, lanes) == tiled(lane16, rows, lanes)
    return jnp.where(same, jnp.bfloat16(1), jnp.bfloat16(0))


def sum_mask(row, rows16, scale=None):
    count, length = (rows16.shape[0], row.shape[1])
    targets = jnp.broadcast_to(row, (16, length)).astype(jnp.int16)
    same = tiled(rows16, count, length) == tiled(targets, count, length)
    if scale is None:
        here = jnp.bfloat16(1)
    else:
        here = tiled(jnp.broadcast_to(scale, (16, length)).astype(jnp.bfloat16), count, length)
    return jnp.where(same, here, jnp.bfloat16(0))


def dot(a, b):
    return jnp.dot(a, b, preferred_element_type=jnp.float32)


def block_index(meets, reach):
    return reach if meets is None else block_for(meets, reach)


def pick_kernel(groups, index_ref, table_ref, *refs):
    out_refs = refs[-len(groups) :]
    lanes = lane_iota(table_ref.shape[0])
    reach = index_ref.shape[0] // 2
    for group, out_ref in zip(groups, out_refs):
        for place, meets in enumerate(group):
            col = column(index_ref[block_index(meets, reach)]).astype(jnp.int16)
            out_ref[place] = dot(pick_mask(col, lanes), table_ref[...]).astype(jnp.bfloat16)


def pick(groups, g2m_src, grid_latent, after=()):
    capacity = g2m_src.shape[2]
    rows, channels = grid_latent.shape
    return call(
        functools.partial(pick_kernel, groups),
        [shape((len(group), capacity, channels)) for group in groups],
        [g2m_src, grid_latent, *after],
        2 * sum(map(len, groups)) * capacity * rows * channels,
    )


def first_pick_kernel(groups, parts, index_hbm, table_hbm, *refs):
    out_refs, (index_ref, table_ref, index_sem, table_sems) = (refs[: len(groups)], refs[len(groups) :])
    rows = table_ref.shape[0] // parts
    index_copy = pltpu.make_async_copy(index_hbm, index_ref, index_sem)
    index_copy.start()
    copies = []
    for part in range(parts):
        here = pl.ds(part * rows, rows)
        copies.append(pltpu.make_async_copy(table_hbm.at[here, :], table_ref.at[here, :], table_sems.at[part]))
        copies[-1].start()
    index_copy.wait()
    reach = index_ref.shape[0] // 2
    cols = [
        column(index_ref[block_index(meets, reach)]).astype(jnp.int16) for group in groups for meets in group
    ]
    totals = [None] * len(cols)
    for part, copy in enumerate(copies):
        copy.wait()
        lanes = (lane_iota(rows).astype(jnp.int32) + part * rows).astype(jnp.int16)
        for k, col in enumerate(cols):
            found = dot(pick_mask(col, lanes), table_ref[pl.ds(part * rows, rows), :])
            totals[k] = found if part == 0 else totals[k] + found
    for group, out_ref in zip(groups, out_refs):
        for place in range(len(group)):
            out_ref[place] = totals.pop(0).astype(jnp.bfloat16)


def first_pick(groups, g2m_src, grid_latent):
    capacity = g2m_src.shape[2]
    rows, channels = grid_latent.shape
    parts = 4
    outputs = [shape((len(group), capacity, channels)) for group in groups]
    outputs += [shape(g2m_src.shape, g2m_src.dtype), shape(grid_latent.shape, grid_latent.dtype)]
    *picked, index, table = pl.pallas_call(
        functools.partial(first_pick_kernel, groups, parts),
        out_shape=[made_in_vmem(o) for o in outputs],
        in_specs=[pl.BlockSpec(memory_space=pl.ANY)] * 2,
        out_specs=[pl.BlockSpec(memory_space=pltpu.VMEM)] * len(outputs),
        scratch_shapes=[pltpu.SemaphoreType.DMA, pltpu.SemaphoreType.DMA((parts,))],
        compiler_params=pltpu.CompilerParams(vmem_limit_bytes=VMEM_BYTES),
    )(taken_from_hbm(g2m_src), taken_from_hbm(grid_latent))
    return picked, index, table


def fetch_kernel(after_ref, *refs):
    count = (len(refs) - 3) // 2
    sources, copied, (source_col_ref, target_col_ref, sems) = (
        refs[:count],
        refs[count : 2 * count],
        refs[2 * count :],
    )
    copies = [pltpu.make_async_copy(sources[k], copied[k], sems.at[k]) for k in range(count)]
    for copy in copies:
        copy.start()
    for copy, row_ref, out_ref in zip(copies, copied, (source_col_ref, target_col_ref)):
        copy.wait()
        out_ref[...] = column(row_ref[...]).astype(jnp.int16)
    for copy in copies[2:]:
        copy.wait()


def fetch(after, *arrays):
    outputs = [shape(a.shape, a.dtype) for a in arrays]
    outputs += [shape((a.shape[1], 128), jnp.int16) for a in arrays[:2]]
    return pl.pallas_call(
        fetch_kernel,
        out_shape=[made_in_vmem(o) for o in outputs],
        in_specs=[pl.BlockSpec(memory_space=pltpu.VMEM)] + [pl.BlockSpec(memory_space=pl.ANY)] * len(arrays),
        out_specs=[pl.BlockSpec(memory_space=pltpu.VMEM)] * len(outputs),
        scratch_shapes=[pltpu.SemaphoreType.DMA((len(arrays),))],
        compiler_params=pltpu.CompilerParams(vmem_limit_bytes=VMEM_BYTES),
    )(taken_from_vmem(after), *[taken_from_hbm(a) for a in arrays])


def encode_kernel(group, others, weight_ref, coef_ref, target_ref, *refs):
    sources, outs = (refs[: others + 1], refs[-len(group) :])
    capacity, channels = sources[0].shape[1:]
    weights = own_and_others_rows(weight_ref, channels, others)
    line = lax.broadcasted_iota(jnp.int32, (PAD, channels), 0)
    pieces = capacity // channels
    reach = coef_ref.shape[0] // 2
    for place, meets in enumerate(group):
        j = block_index(meets, reach)
        projected = dot(sources[0][place], weights[0])
        for source, weight in zip(sources[1:], weights[1:]):
            projected += dot(source[place], weight)
        scale = tiled(column(coef_ref[j]), capacity, channels)
        outs[place][pl.ds(0, capacity), :] = (scale * silu(projected)).astype(jnp.bfloat16)
        target = target_ref[j]
        code = jnp.zeros((PAD, channels), jnp.float32)
        for number, part in enumerate((target >> 3, target & 7)):
            part = part.astype(jnp.float32)
            for piece in range(pieces):
                values = part[:, piece * channels : (piece + 1) * channels]
                code = jnp.where(line == number * pieces + piece, values, code)
        outs[place][pl.ds(capacity, PAD), :] = code.astype(jnp.bfloat16)


def encode(group, picked, arrived, enc_weight, g2m_coef, g2m_dst, after=()):
    count, capacity, channels = picked.shape
    return call(
        functools.partial(encode_kernel, group, len(arrived)),
        [shape((capacity + PAD, channels))] * count,
        [enc_weight, g2m_coef, g2m_dst, picked, *arrived, *after],
        2 * count * capacity * enc_weight.shape[0] * channels,
        count * capacity * channels,
    )


def gather_in_kernel(before_ref, *refs):
    blocks, out_ref = (refs[:-1], refs[-1])
    nodes, channels = before_ref.shape
    capacity = blocks[0].shape[0] - PAD
    rows16 = row_iota(nodes)
    pieces = capacity // channels
    total = before_ref[...].astype(jnp.float32)
    for block in blocks:
        code = block[pl.ds(capacity, PAD), :].astype(jnp.float32)
        lines = [code[i : i + 1, :] for i in range(2 * pieces)]
        upper = lines[0] if pieces == 1 else jnp.concatenate(lines[:pieces], axis=1)
        lower = lines[1] if pieces == 1 else jnp.concatenate(lines[pieces:], axis=1)
        target = (8.0 * upper + lower).astype(jnp.int32)
        total += dot(sum_mask(target, rows16), block[pl.ds(0, capacity), :])
    out_ref[...] = total.astype(out_ref.dtype)


def gather_in(before, blocks, dtype):
    nodes, channels = before.shape
    slots = len(blocks) * blocks[0].shape[0]
    return call(
        gather_in_kernel,
        [shape((nodes, channels), dtype)],
        [before, *blocks],
        2 * nodes * slots * channels,
    )[0]


def list_kernel(reach, listed_ref, state_ref, one_ref, two_ref, far_ref, near_ref):
    nodes = state_ref.shape[0]
    width = listed_ref.shape[2]
    lanes = lane_iota(nodes)
    region = lax.axis_index(REGION)
    core = region % 2
    wanted = [
        meets(region) - core + i - region for meets in (meets_two, meets_other_two) for i in range(2)
    ]
    wanted += [meets_other_three(region) - region, meets_core(region) - region]
    wanted = [offset + reach - jnp.where(offset > 0, 1, 0) for offset in wanted]
    for k in range(0, len(wanted), 2):
        row = jnp.concatenate([listed_ref[wanted[k + i]] for i in range(2)], axis=1)
        rows = dot(pick_mask(column(row).astype(jnp.int16), lanes), state_ref[...])
        rows = rows.astype(jnp.bfloat16)
        parts = [rows[i * width : (i + 1) * width] for i in range(2)]
        if k < 4:
            ref = one_ref if k == 0 else two_ref
            for i in range(2):
                ref[i] = parts[i]
        else:
            far_ref[...] = parts[0]
            near_ref[...] = parts[1]


def list_rows(state, halo_send, reach):
    nodes, channels = state.shape
    links, unused, width = halo_send.shape
    one, two = [shape(d) for d in ((width, channels), (2, width, channels))]
    return call(
        functools.partial(list_kernel, reach),
        [two, two, one, one],
        [halo_send, state],
        0,
    )


def forward_kernel(near_ref, one_ref, two_ref, out_ref):
    other = 1 - lax.axis_index("edge")
    out_ref[0] = near_ref[...]
    out_ref[1] = one_ref[other]
    out_ref[2] = two_ref[other]


def order_kernel(one_ref, two_ref, distant_ref, across_ref, out_ref):
    width = distant_ref.shape[0]
    region = lax.axis_index(REGION)
    core = region % 2
    low_even = region // 2 % 2 == 0
    own = (one_ref[core], two_ref[core])
    across = (across_ref[1], across_ref[2])
    before, after = [
        [jnp.where(low_even == first, pair[0], pair[1]) for pair in (own, across)] for first in (False, True)
    ]
    near = across_ref[0]
    distant = distant_ref[...]
    even = core == 0
    rows = (
        jnp.where(even, after[1], distant),
        after[0],
        jnp.where(even, near, after[1]),
        jnp.where(even, before[1], near),
        before[0],
        jnp.where(even, distant, before[1]),
    )
    for j, part in enumerate(rows):
        out_ref[pl.ds(j * width, width), :] = part


def exchange_listed(one, two, far, near):
    width, channels = near.shape
    one, two = swapped(one, meets_two), swapped(two, meets_other_two)
    distant = swapped(far, meets_other_three)
    sent = call(forward_kernel, [shape((3, width, channels))], [near, one, two], 0)[0]
    across = swapped(sent, meets_core)
    return call(
        order_kernel, [shape((6 * width, channels))], [one, two, distant, across], 0
    )[0]


def projected_rows(weight_ref, parts):
    weights = own_and_others_rows(weight_ref, parts[0].shape[1], len(parts) - 1)
    total = dot(parts[0][...], weights[0])
    for part, weight in zip(parts[1:], weights[1:]):
        total += dot(part[...], weight)
    return total.astype(jnp.bfloat16)


def project_kernel(layer, src_ref, dst_ref, *refs):
    states, table_ref = (refs[:-1], refs[-1])
    nodes = states[0].shape[0]
    table_ref[pl.ds(0, nodes), :] = projected_rows(src_ref.at[layer], states)
    table_ref[pl.ds(nodes, nodes), :] = projected_rows(dst_ref.at[layer], states)


def project(layer, states, src_weights, dst_weights):
    nodes, channels = states[0].shape
    depth = src_weights.shape[1]
    return call(
        functools.partial(project_kernel, layer),
        [shape((2 * nodes, channels))],
        [src_weights, dst_weights, *states],
        4 * nodes * depth * channels,
    )[0]


def first_kernel(turn, source_ref, target_ref, table_ref, out_ref):
    lanes = lane_iota(table_ref.shape[0] // 2)
    for start in range(0, source_ref.shape[0], turn):
        here = pl.ds(start, turn)
        mask = jnp.concatenate(
            [pick_mask(source_ref[here, :], lanes), pick_mask(target_ref[here, :], lanes)], axis=1
        )
        out_ref[here, :] = dot(mask, table_ref[...])


def first_part(source_col, target_col, table):
    rows, channels = table.shape
    edges = source_col.shape[0]
    return call(
        functools.partial(first_kernel, 512),
        [shape((edges, channels), jnp.float32)],
        [source_col, target_col, table],
        2 * edges * rows * channels,
    )[0]


def message_kernel(turn, layer, source_ref, target_ref, coef_ref, state_ref, first_ref, weight_ref, *refs):
    listed, (out_ref, message_ref) = (refs[:-2], refs[-2:])
    nodes, channels = state_ref.shape
    table = projected_rows(weight_ref.at[layer], listed)
    lanes = (lane_iota(table.shape[0]).astype(jnp.int32) + nodes).astype(jnp.int16)
    rows16 = row_iota(nodes)
    total = state_ref[...].astype(jnp.float32)
    edges = source_ref.shape[0]

    def gathered(start):
        here = pl.ds(start, turn)
        return first_ref[here, :] + dot(pick_mask(source_ref[here, :], lanes), table)

    ahead = gathered(0)
    for start in range(0, edges, turn):
        here = pl.ds(start, turn)
        summed = ahead
        if start + turn < edges:
            ahead = gathered(start + turn)
        message_ref[here, :] = silu(summed).astype(jnp.bfloat16)
        mask = sum_mask(target_ref[:, here], rows16, coef_ref[:, here])
        total += dot(mask, message_ref[here, :])
    out_ref[...] = total.astype(jnp.bfloat16)


def messages(layer, source_col, m2m_dst, m2m_coef, state, first, src_weights, listed, final):
    nodes, channels = state.shape
    edges = m2m_dst.shape[1]
    named = listed[0].shape[0]
    return call(
        functools.partial(message_kernel, 512, layer),
        [shape((nodes, channels))],
        [source_col, m2m_dst, m2m_coef, state, first, src_weights, *listed],
        2 * edges * (named + nodes) * channels,
        edges * channels,
        [pltpu.VMEM((edges, channels), jnp.bfloat16)],
        final,
    )[0]


def on_device(
    grid_latent,
    enc_weight,
    mesh_latent,
    g2m_src,
    g2m_dst,
    g2m_coef,
    src_weights,
    dst_weights,
    halo_send,
    m2m_src,
    m2m_dst,
    m2m_coef,
):
    reach = (g2m_src.shape[1] - 1) // 2
    assert reach == 3 and lax.axis_size("edge") == 2
    g2m_src, g2m_dst, g2m_coef, halo_send = [
        jnp.swapaxes(a, 0, 1) for a in (g2m_src, g2m_dst, g2m_coef, halo_send)
    ]
    groups = [
        (meets_three,), (meets_other_three,), (meets_two, meets_other_two), (meets_next, None), (meets_core,)
    ]
    picked, g2m_src, grid_latent = first_pick(groups[:2], g2m_src, grid_latent)
    arrived = [from_others(rows, group[0]) for group, rows in zip(groups, picked)]
    m2m_src, m2m_dst, m2m_coef, enc_weight, g2m_coef, g2m_dst, mesh_latent, halo_send, src_weights, dst_weights, *cols = (
        fetch(
            g2m_src, m2m_src, m2m_dst, m2m_coef, enc_weight, g2m_coef, g2m_dst, mesh_latent, halo_send,
            src_weights, dst_weights,
        )
    )
    source_col, target_col = cols

    def pick_next(place, after):
        picked.extend(pick(groups[place : place + 1], g2m_src, grid_latent, after))
        arrived.append(from_others(picked[place]))

    def encode_group(place, after=()):
        return encode(groups[place], picked[place], arrived[place], enc_weight, g2m_coef, g2m_dst, after)

    pick_next(2, arrived[0])
    encoded = encode_group(0) + encode_group(1)
    pick_next(3, encoded)
    encoded += encode_group(2)
    blocks = [swapped(block, meets) for block, meets in zip(encoded, groups[0] + groups[1] + groups[2])]
    state = gather_in(mesh_latent, blocks[:2], jnp.float32)
    pick_next(4, [state, *encoded[2:]])
    following, own = encode_group(3)
    (near,) = encode_group(4)
    blocks.append(swapped(following, meets_next))
    near = swapped(near, meets_core)
    state = gather_in(state, blocks[2:4] + [own], jnp.float32)
    state = gather_in(state, [blocks[4], near], jnp.bfloat16)
    layers = src_weights.shape[0]
    for layer in range(layers):
        others = from_others(state)
        listed = exchange_listed(*list_rows(state, halo_send, reach))
        table = project(layer, [state, *others], src_weights, dst_weights)
        listed = [listed, *from_others(listed)]
        first = first_part(source_col, target_col, table)
        state = messages(
            layer, source_col, m2m_dst, m2m_coef, state, first, src_weights, listed, layer == layers - 1
        )
    return state


def solution(mesh):
    placed = (
        P(("groups", "space", "edge"), "feat"),
        P(None, "feat"),
        P(("groups", "space", "edge"), "feat"),
        P(("groups", "space", "edge"), None, None),
        P(("groups", "space", "edge"), None, None),
        P(("groups", "space", "edge"), None, None),
        P(None, None, "feat"),
        P(None, None, "feat"),
        P(("groups", "space", "edge"), None, None),
        P(("groups", "space", "edge"), None),
        P(("groups", "space", "edge"), None),
        P(("groups", "space", "edge"), None),
    )
    return jax.shard_map(
        on_device,
        mesh=mesh,
        in_specs=placed,
        out_specs=P(("groups", "space", "edge"), "feat"),
        check_vma=False,
    )
```

```python
import functools

import jax
import jax.numpy as jnp
from jax import lax
from jax.experimental import pallas as pl
from jax.experimental.pallas import tpu as pltpu
from jax.sharding import PartitionSpec as P

REGION = ("space", "edge")
PAD = 16
VMEM_BYTES = 28 * 1024 * 1024


def made_in_vmem(output):
    return pltpu.VMEM(output.shape, output.dtype)


def taken_from_vmem(array):
    return pltpu.with_memory_space_constraint(array, pltpu.VMEM)


def taken_from_hbm(array):
    return pltpu.with_memory_space_constraint(array, pltpu.HBM)


def call(kernel, outputs, inputs, flops, transcendentals=0, scratch=(), final=False, fetched=0):
    size = lambda a: int(a.size) * a.dtype.itemsize
    shapes = outputs if final else [made_in_vmem(o) for o in outputs]
    return pl.pallas_call(
        kernel,
        out_shape=shapes,
        in_specs=[pl.BlockSpec(memory_space=pltpu.VMEM)] * len(inputs),
        out_specs=[pl.BlockSpec(memory_space=pltpu.VMEM)] * len(outputs),
        scratch_shapes=list(scratch),
        compiler_params=pltpu.CompilerParams(vmem_limit_bytes=VMEM_BYTES),
        cost_estimate=pl.CostEstimate(
            flops=flops,
            bytes_accessed=sum(size(a) for a in list(inputs) + list(outputs)) if flops else 0,
            transcendentals=transcendentals,
        ),
    )(*inputs[:fetched], *[taken_from_vmem(a) for a in inputs[fetched:]])


def shape(dims, dtype=jnp.bfloat16):
    return jax.ShapeDtypeStruct(dims, dtype)


def meets_core(r):
    return r + 1 - 2 * (r % 2)


def meets_next(r):
    return r - 1 + 2 * (r % 2)


def meets_two(r):
    return r + 2 - 4 * (r // 2 % 2)


def meets_other_two(r):
    return r - 2 + 4 * (r // 2 % 2)


def meets_three(r):
    return r + 3 - 6 * (r % 2)


def meets_other_three(r):
    return r - 3 + 6 * (r % 2)


def pairs(meets):
    count = lax.axis_size(REGION)
    return [(r, meets(r)) for r in range(count) if 0 <= meets(r) < count]


def swapped(value, meets):
    return lax.ppermute(value, REGION, pairs(meets))


def block_for(meets, reach):
    region = lax.axis_index(REGION)
    return meets(region) - region + reach


def from_others(value, meets=None):
    n = lax.axis_size("feat")
    if meets is None:
        axes, rings = ("feat", [[i for i in range(n)]])
    else:
        axes, cores = (("space", "feat", "edge"), lax.axis_size("edge"))
        rings = [
            [(r // cores * n + i) * cores + r % cores for i in range(n)] for r, unused in pairs(meets)
        ]
    return [
        lax.ppermute(value, axes, [(ring[i], ring[(i + k) % n]) for ring in rings for i in range(n)])
        for k in range(1, n)
    ]


def own_and_others_rows(weight_ref, channels, others):
    n = others + 1
    me = lax.axis_index("feat")
    blocks = []
    for k in range(n):
        owner = lax.rem(me - k + n, n)
        start = pl.multiple_of(owner * channels, channels)
        blocks.append(weight_ref[pl.ds(start, channels), :])
    return blocks


def silu(v):
    half = 0.5 * v
    return half + half * jnp.tanh(half)


def column(row):
    length = row.shape[1]
    parts = [
        jnp.broadcast_to(row[:, c * 128 : (c + 1) * 128], (128, 128)).T for c in range(length // 128)
    ]
    return parts[0] if len(parts) == 1 else jnp.concatenate(parts, axis=0)


def lane_iota(count):
    return lax.broadcasted_iota(jnp.int32, (16, count), 1).astype(jnp.int16)


def row_iota(count):
    return lax.broadcasted_iota(jnp.int32, (count, 128), 0).astype(jnp.int16)


def tiled(value, rows, lanes):
    if value.shape[0] != rows:
        value = jnp.concatenate([value] * (rows // value.shape[0]), axis=0)
    if value.shape[1] != lanes:
        value = jnp.concatenate([value] * (lanes // value.shape[1]), axis=1)
    return value


def pick_mask(column16, lane16):
    rows, lanes = (column16.shape[0], lane16.shape[1])
    same = tiled(column16, rows, lanes) == tiled(lane16, rows, lanes)
    return jnp.where(same, jnp.bfloat16(1), jnp.bfloat16(0))


def sum_mask(row, rows16, scale=None):
    count, length = (rows16.shape[0], row.shape[1])
    targets = jnp.broadcast_to(row, (16, length)).astype(jnp.int16)
    same = tiled(rows16, count, length) == tiled(targets, count, length)
    if scale is None:
        here = jnp.bfloat16(1)
    else:
        here = tiled(jnp.broadcast_to(scale, (16, length)).astype(jnp.bfloat16), count, length)
    return jnp.where(same, here, jnp.bfloat16(0))


def dot(a, b):
    return jnp.dot(a, b, preferred_element_type=jnp.float32)


def block_index(meets, reach):
    return reach if meets is None else block_for(meets, reach)


def pick_kernel(groups, index_ref, table_ref, *refs):
    out_refs = refs[-len(groups) :]
    lanes = lane_iota(table_ref.shape[0])
    reach = index_ref.shape[0] // 2
    for group, out_ref in zip(groups, out_refs):
        for place, meets in enumerate(group):
            col = column(index_ref[block_index(meets, reach)]).astype(jnp.int16)
            out_ref[place] = dot(pick_mask(col, lanes), table_ref[...]).astype(jnp.bfloat16)


def pick(groups, g2m_src, grid_latent, after=()):
    capacity = g2m_src.shape[2]
    rows, channels = grid_latent.shape
    return call(
        functools.partial(pick_kernel, groups),
        [shape((len(group), capacity, channels)) for group in groups],
        [g2m_src, grid_latent, *after],
        2 * sum(map(len, groups)) * capacity * rows * channels,
    )


def first_pick_kernel(groups, parts, index_hbm, table_hbm, *refs):
    out_refs, (index_ref, table_ref, index_sem, table_sems) = (refs[: len(groups)], refs[len(groups) :])
    rows = table_ref.shape[0] // parts
    index_copy = pltpu.make_async_copy(index_hbm, index_ref, index_sem)
    index_copy.start()
    copies = []
    for part in range(parts):
        here = pl.ds(part * rows, rows)
        copies.append(pltpu.make_async_copy(table_hbm.at[here, :], table_ref.at[here, :], table_sems.at[part]))
        copies[-1].start()
    index_copy.wait()
    reach = index_ref.shape[0] // 2
    cols = [
        column(index_ref[block_index(meets, reach)]).astype(jnp.int16) for group in groups for meets in group
    ]
    totals = [None] * len(cols)
    for part, copy in enumerate(copies):
        copy.wait()
        lanes = (lane_iota(rows).astype(jnp.int32) + part * rows).astype(jnp.int16)
        for k, col in enumerate(cols):
            found = dot(pick_mask(col, lanes), table_ref[pl.ds(part * rows, rows), :])
            totals[k] = found if part == 0 else totals[k] + found
    for group, out_ref in zip(groups, out_refs):
        for place in range(len(group)):
            out_ref[place] = totals.pop(0).astype(jnp.bfloat16)


def first_pick(groups, g2m_src, grid_latent):
    capacity = g2m_src.shape[2]
    rows, channels = grid_latent.shape
    parts = 4
    outputs = [shape((len(group), capacity, channels)) for group in groups]
    outputs += [shape(g2m_src.shape, g2m_src.dtype), shape(grid_latent.shape, grid_latent.dtype)]
    *picked, index, table = pl.pallas_call(
        functools.partial(first_pick_kernel, groups, parts),
        out_shape=[made_in_vmem(o) for o in outputs],
        in_specs=[pl.BlockSpec(memory_space=pl.ANY)] * 2,
        out_specs=[pl.BlockSpec(memory_space=pltpu.VMEM)] * len(outputs),
        scratch_shapes=[pltpu.SemaphoreType.DMA, pltpu.SemaphoreType.DMA((parts,))],
        compiler_params=pltpu.CompilerParams(vmem_limit_bytes=VMEM_BYTES),
    )(taken_from_hbm(g2m_src), taken_from_hbm(grid_latent))
    return picked, index, table


def fetch_kernel(after_ref, *refs):
    count = (len(refs) - 3) // 2
    sources, copied, (source_col_ref, target_col_ref, sems) = (
        refs[:count],
        refs[count : 2 * count],
        refs[2 * count :],
    )
    copies = [pltpu.make_async_copy(sources[k], copied[k], sems.at[k]) for k in range(count)]
    for copy in copies:
        copy.start()
    for copy, row_ref, out_ref in zip(copies, copied, (source_col_ref, target_col_ref)):
        copy.wait()
        out_ref[...] = column(row_ref[...]).astype(jnp.int16)
    for copy in copies[2:]:
        copy.wait()


def fetch(after, *arrays):
    outputs = [shape(a.shape, a.dtype) for a in arrays]
    outputs += [shape((a.shape[1], 128), jnp.int16) for a in arrays[:2]]
    return pl.pallas_call(
        fetch_kernel,
        out_shape=[made_in_vmem(o) for o in outputs],
        in_specs=[pl.BlockSpec(memory_space=pltpu.VMEM)] + [pl.BlockSpec(memory_space=pl.ANY)] * len(arrays),
        out_specs=[pl.BlockSpec(memory_space=pltpu.VMEM)] * len(outputs),
        scratch_shapes=[pltpu.SemaphoreType.DMA((len(arrays),))],
        compiler_params=pltpu.CompilerParams(vmem_limit_bytes=VMEM_BYTES),
    )(taken_from_vmem(after), *[taken_from_hbm(a) for a in arrays])


def encode_kernel(group, others, weight_ref, coef_ref, target_ref, *refs):
    sources, outs = (refs[: others + 1], refs[-len(group) :])
    capacity, channels = sources[0].shape[1:]
    weights = own_and_others_rows(weight_ref, channels, others)
    line = lax.broadcasted_iota(jnp.int32, (PAD, channels), 0)
    pieces = capacity // channels
    reach = coef_ref.shape[0] // 2
    for place, meets in enumerate(group):
        j = block_index(meets, reach)
        projected = dot(sources[0][place], weights[0])
        for source, weight in zip(sources[1:], weights[1:]):
            projected += dot(source[place], weight)
        scale = tiled(column(coef_ref[j]), capacity, channels)
        outs[place][pl.ds(0, capacity), :] = (scale * silu(projected)).astype(jnp.bfloat16)
        target = target_ref[j]
        code = jnp.zeros((PAD, channels), jnp.float32)
        for number, part in enumerate((target >> 3, target & 7)):
            part = part.astype(jnp.float32)
            for piece in range(pieces):
                values = part[:, piece * channels : (piece + 1) * channels]
                code = jnp.where(line == number * pieces + piece, values, code)
        outs[place][pl.ds(capacity, PAD), :] = code.astype(jnp.bfloat16)


def encode(group, picked, arrived, enc_weight, g2m_coef, g2m_dst, after=()):
    count, capacity, channels = picked.shape
    return call(
        functools.partial(encode_kernel, group, len(arrived)),
        [shape((capacity + PAD, channels))] * count,
        [enc_weight, g2m_coef, g2m_dst, picked, *arrived, *after],
        2 * count * capacity * enc_weight.shape[0] * channels,
        count * capacity * channels,
    )


def gather_in_kernel(before_ref, *refs):
    blocks, out_ref = (refs[:-1], refs[-1])
    nodes, channels = before_ref.shape
    capacity = blocks[0].shape[0] - PAD
    rows16 = row_iota(nodes)
    pieces = capacity // channels
    total = before_ref[...].astype(jnp.float32)
    for block in blocks:
        code = block[pl.ds(capacity, PAD), :].astype(jnp.float32)
        lines = [code[i : i + 1, :] for i in range(2 * pieces)]
        upper = lines[0] if pieces == 1 else jnp.concatenate(lines[:pieces], axis=1)
        lower = lines[1] if pieces == 1 else jnp.concatenate(lines[pieces:], axis=1)
        target = (8.0 * upper + lower).astype(jnp.int32)
        total += dot(sum_mask(target, rows16), block[pl.ds(0, capacity), :])
    out_ref[...] = total.astype(out_ref.dtype)


def gather_in(before, blocks, dtype):
    nodes, channels = before.shape
    slots = len(blocks) * blocks[0].shape[0]
    return call(
        gather_in_kernel,
        [shape((nodes, channels), dtype)],
        [before, *blocks],
        2 * nodes * slots * channels,
    )[0]


def list_kernel(reach, listed_ref, state_ref, far_ref, near_ref, one_ref, two_ref):
    nodes = state_ref.shape[0]
    width = listed_ref.shape[2]
    lanes = lane_iota(nodes)
    region = lax.axis_index(REGION)
    core = region % 2
    wanted = [
        meets(region) - core + i - region for meets in (meets_two, meets_other_two) for i in range(2)
    ]
    wanted += [meets_other_three(region) - region, meets_core(region) - region]
    wanted = [offset + reach - jnp.where(offset > 0, 1, 0) for offset in wanted]
    for k in range(0, len(wanted), 2):
        row = jnp.concatenate([listed_ref[wanted[k + i]] for i in range(2)], axis=1)
        rows = dot(pick_mask(column(row).astype(jnp.int16), lanes), state_ref[...])
        rows = rows.astype(jnp.bfloat16)
        parts = [rows[i * width : (i + 1) * width] for i in range(2)]
        if k < 4:
            ref = one_ref if k == 0 else two_ref
            for i in range(2):
                ref[i] = parts[i]
        else:
            far_ref[pl.ds(0, width), :] = parts[0]
            far_ref[pl.ds(width, far_ref.shape[0] - width), :] = jnp.zeros(
                (far_ref.shape[0] - width, parts[0].shape[1]), jnp.bfloat16
            )
            near_ref[...] = parts[1]


def list_rows(state, halo_send, reach):
    nodes, channels = state.shape
    links, unused, width = halo_send.shape
    one, two = [shape(d) for d in ((width, channels), (2, width, channels))]
    far = shape((2 * width + PAD, channels))
    return call(
        functools.partial(list_kernel, reach),
        [far, one, two, two],
        [halo_send, state],
        0,
    )


def forward_kernel(distant_ref, near_ref, one_ref, two_ref, out_ref):
    other = 1 - lax.axis_index("edge")
    out_ref[0] = near_ref[...]
    out_ref[1] = one_ref[other]
    out_ref[2] = two_ref[other]


def order_kernel(distant_ref, one_ref, two_ref, across_ref, out_ref):
    width = across_ref.shape[1]
    region = lax.axis_index(REGION)
    core = region % 2
    low_even = region // 2 % 2 == 0
    own = (one_ref[core], two_ref[core])
    across = (across_ref[1], across_ref[2])
    before, after = [
        [jnp.where(low_even == first, pair[0], pair[1]) for pair in (own, across)] for first in (False, True)
    ]
    near = across_ref[0]
    distant = distant_ref[pl.ds(0, width), :]
    even = core == 0
    rows = (
        jnp.where(even, after[1], distant),
        after[0],
        jnp.where(even, near, after[1]),
        jnp.where(even, before[1], near),
        before[0],
        jnp.where(even, distant, before[1]),
    )
    for j, part in enumerate(rows):
        out_ref[pl.ds(j * width, width), :] = part


def exchange_listed(far, near, one, two):
    width, channels = near.shape
    distant = swapped(far, meets_other_three)
    one, two = swapped(one, meets_two), swapped(two, meets_other_two)
    sent = call(forward_kernel, [shape((3, width, channels))], [distant, near, one, two], 0)[0]
    across = swapped(sent, meets_core)
    return call(
        order_kernel, [shape((6 * width, channels))], [distant, one, two, across], 0
    )[0]


def projected_rows(weight_ref, parts):
    weights = own_and_others_rows(weight_ref, parts[0].shape[1], len(parts) - 1)
    total = dot(parts[0][...], weights[0])
    for part, weight in zip(parts[1:], weights[1:]):
        total += dot(part[...], weight)
    return total.astype(jnp.bfloat16)


def project_kernel(layer, src_ref, dst_ref, *refs):
    states, table_ref = (refs[:-1], refs[-1])
    nodes = states[0].shape[0]
    table_ref[pl.ds(0, nodes), :] = projected_rows(src_ref.at[layer], states)
    table_ref[pl.ds(nodes, nodes), :] = projected_rows(dst_ref.at[layer], states)


def project(layer, states, src_weights, dst_weights):
    nodes, channels = states[0].shape
    depth = src_weights.shape[1]
    return call(
        functools.partial(project_kernel, layer),
        [shape((2 * nodes, channels))],
        [src_weights, dst_weights, *states],
        4 * nodes * depth * channels,
    )[0]


def first_kernel(turn, source_ref, target_ref, table_ref, out_ref):
    lanes = lane_iota(table_ref.shape[0] // 2)
    for start in range(0, source_ref.shape[0], turn):
        here = pl.ds(start, turn)
        mask = jnp.concatenate(
            [pick_mask(source_ref[here, :], lanes), pick_mask(target_ref[here, :], lanes)], axis=1
        )
        out_ref[here, :] = dot(mask, table_ref[...])


def first_part(source_col, target_col, table):
    rows, channels = table.shape
    edges = source_col.shape[0]
    return call(
        functools.partial(first_kernel, 512),
        [shape((edges, channels), jnp.float32)],
        [source_col, target_col, table],
        2 * edges * rows * channels,
    )[0]


def message_kernel(turn, layer, source_ref, target_ref, coef_ref, state_ref, first_ref, weight_ref, *refs):
    listed, (out_ref, message_ref) = (refs[:-2], refs[-2:])
    nodes, channels = state_ref.shape
    table = projected_rows(weight_ref.at[layer], listed)
    lanes = (lane_iota(table.shape[0]).astype(jnp.int32) + nodes).astype(jnp.int16)
    rows16 = row_iota(nodes)
    total = state_ref[...].astype(jnp.float32)
    edges = source_ref.shape[0]

    def gathered(start):
        here = pl.ds(start, turn)
        return first_ref[here, :] + dot(pick_mask(source_ref[here, :], lanes), table)

    ahead = gathered(0)
    for start in range(0, edges, turn):
        here = pl.ds(start, turn)
        summed = ahead
        if start + turn < edges:
            ahead = gathered(start + turn)
        message_ref[here, :] = silu(summed).astype(jnp.bfloat16)
        mask = sum_mask(target_ref[:, here], rows16, coef_ref[:, here])
        total += dot(mask, message_ref[here, :])
    out_ref[...] = total.astype(jnp.bfloat16)


def messages(layer, source_col, m2m_dst, m2m_coef, state, first, src_weights, listed, final):
    nodes, channels = state.shape
    edges = m2m_dst.shape[1]
    named = listed[0].shape[0]
    return call(
        functools.partial(message_kernel, 512, layer),
        [shape((nodes, channels))],
        [source_col, m2m_dst, m2m_coef, state, first, src_weights, *listed],
        2 * edges * (named + nodes) * channels,
        edges * channels,
        [pltpu.VMEM((edges, channels), jnp.bfloat16)],
        final,
    )[0]


def on_device(
    grid_latent,
    enc_weight,
    mesh_latent,
    g2m_src,
    g2m_dst,
    g2m_coef,
    src_weights,
    dst_weights,
    halo_send,
    m2m_src,
    m2m_dst,
    m2m_coef,
):
    reach = (g2m_src.shape[1] - 1) // 2
    assert reach == 3 and lax.axis_size("edge") == 2
    g2m_src, g2m_dst, g2m_coef, halo_send = [
        jnp.swapaxes(a, 0, 1) for a in (g2m_src, g2m_dst, g2m_coef, halo_send)
    ]
    groups = [
        (meets_other_three,), (meets_three,), (meets_two, meets_other_two), (meets_next, None), (meets_core,)
    ]
    picked, g2m_src, grid_latent = first_pick(groups[:2], g2m_src, grid_latent)
    arrived = [from_others(rows, group[0]) for group, rows in zip(groups, picked)]
    m2m_src, m2m_dst, m2m_coef, enc_weight, g2m_coef, g2m_dst, mesh_latent, halo_send, src_weights, dst_weights, *cols = (
        fetch(
            g2m_src, m2m_src, m2m_dst, m2m_coef, enc_weight, g2m_coef, g2m_dst, mesh_latent, halo_send,
            src_weights, dst_weights,
        )
    )
    source_col, target_col = cols

    def pick_next(place, after):
        picked.extend(pick(groups[place : place + 1], g2m_src, grid_latent, after))
        arrived.append(from_others(picked[place]))

    def encode_group(place, after=()):
        return encode(groups[place], picked[place], arrived[place], enc_weight, g2m_coef, g2m_dst, after)

    pick_next(2, [*arrived[0], source_col])
    encoded = encode_group(0) + encode_group(1)
    pick_next(3, encoded)
    encoded += encode_group(2)
    blocks = [swapped(block, meets) for block, meets in zip(encoded, groups[0] + groups[1] + groups[2])]
    state = gather_in(mesh_latent, blocks[:2], jnp.float32)
    pick_next(4, [state, *encoded[2:]])
    following, own = encode_group(3)
    (near,) = encode_group(4)
    blocks.append(swapped(following, meets_next))
    near = swapped(near, meets_core)
    state = gather_in(state, blocks[2:4] + [own], jnp.float32)
    state = gather_in(state, [blocks[4], near], jnp.bfloat16)
    layers = src_weights.shape[0]
    for layer in range(layers):
        others = from_others(state)
        listed = exchange_listed(*list_rows(state, halo_send, reach))
        table = project(layer, [state, *others], src_weights, dst_weights)
        listed = [listed, *from_others(listed)]
        first = first_part(source_col, target_col, table)
        state = messages(
            layer, source_col, m2m_dst, m2m_coef, state, first, src_weights, listed, layer == layers - 1
        )
    return state


def solution(mesh):
    placed = (
        P(("groups", "space", "edge"), "feat"),
        P(None, "feat"),
        P(("groups", "space", "edge"), "feat"),
        P(("groups", "space", "edge"), None, None),
        P(("groups", "space", "edge"), None, None),
        P(("groups", "space", "edge"), None, None),
        P(None, None, "feat"),
        P(None, None, "feat"),
        P(("groups", "space", "edge"), None, None),
        P(("groups", "space", "edge"), None),
        P(("groups", "space", "edge"), None),
        P(("groups", "space", "edge"), None),
    )
    return jax.shard_map(
        on_device,
        mesh=mesh,
        in_specs=placed,
        out_specs=P(("groups", "space", "edge"), "feat"),
        check_vma=False,
    )
```

```python
import functools

import jax
import jax.numpy as jnp
from jax import lax
from jax.experimental import pallas as pl
from jax.experimental.pallas import tpu as pltpu
from jax.sharding import PartitionSpec as P

REGION = ("space", "edge")
PAD = 16
VMEM_BYTES = 28 * 1024 * 1024


def made_in_vmem(output):
    return pltpu.VMEM(output.shape, output.dtype)


def taken_from_vmem(array):
    return pltpu.with_memory_space_constraint(array, pltpu.VMEM)


def taken_from_hbm(array):
    return pltpu.with_memory_space_constraint(array, pltpu.HBM)


def call(kernel, outputs, inputs, flops, transcendentals=0, scratch=(), final=False, fetched=0):
    size = lambda a: int(a.size) * a.dtype.itemsize
    shapes = outputs if final else [made_in_vmem(o) for o in outputs]
    return pl.pallas_call(
        kernel,
        out_shape=shapes,
        in_specs=[pl.BlockSpec(memory_space=pltpu.VMEM)] * len(inputs),
        out_specs=[pl.BlockSpec(memory_space=pltpu.VMEM)] * len(outputs),
        scratch_shapes=list(scratch),
        compiler_params=pltpu.CompilerParams(vmem_limit_bytes=VMEM_BYTES),
        cost_estimate=pl.CostEstimate(
            flops=flops,
            bytes_accessed=sum(size(a) for a in list(inputs) + list(outputs)) if flops else 0,
            transcendentals=transcendentals,
        ),
    )(*inputs[:fetched], *[taken_from_vmem(a) for a in inputs[fetched:]])


def shape(dims, dtype=jnp.bfloat16):
    return jax.ShapeDtypeStruct(dims, dtype)


def meets_core(r):
    return r + 1 - 2 * (r % 2)


def meets_next(r):
    return r - 1 + 2 * (r % 2)


def meets_two(r):
    return r + 2 - 4 * (r // 2 % 2)


def meets_other_two(r):
    return r - 2 + 4 * (r // 2 % 2)


def meets_three(r):
    return r + 3 - 6 * (r % 2)


def meets_other_three(r):
    return r - 3 + 6 * (r % 2)


def pairs(meets):
    count = lax.axis_size(REGION)
    return [(r, meets(r)) for r in range(count) if 0 <= meets(r) < count]


def swapped(value, meets):
    return lax.ppermute(value, REGION, pairs(meets))


def block_for(meets, reach):
    region = lax.axis_index(REGION)
    return meets(region) - region + reach


def from_others(value, meets=None):
    n = lax.axis_size("feat")
    if meets is None:
        axes, rings = ("feat", [[i for i in range(n)]])
    else:
        axes, cores = (("space", "feat", "edge"), lax.axis_size("edge"))
        rings = [
            [(r // cores * n + i) * cores + r % cores for i in range(n)] for r, unused in pairs(meets)
        ]
    return [
        lax.ppermute(value, axes, [(ring[i], ring[(i + k) % n]) for ring in rings for i in range(n)])
        for k in range(1, n)
    ]


def own_and_others_rows(weight_ref, channels, others):
    n = others + 1
    me = lax.axis_index("feat")
    blocks = []
    for k in range(n):
        owner = lax.rem(me - k + n, n)
        start = pl.multiple_of(owner * channels, channels)
        blocks.append(weight_ref[pl.ds(start, channels), :])
    return blocks


def silu(v):
    half = 0.5 * v
    return half + half * jnp.tanh(half)


def column(row):
    length = row.shape[1]
    parts = [
        jnp.broadcast_to(row[:, c * 128 : (c + 1) * 128], (128, 128)).T for c in range(length // 128)
    ]
    return parts[0] if len(parts) == 1 else jnp.concatenate(parts, axis=0)


def lane_iota(count):
    return lax.broadcasted_iota(jnp.int32, (16, count), 1).astype(jnp.int16)


def row_iota(count):
    return lax.broadcasted_iota(jnp.int32, (count, 128), 0).astype(jnp.int16)


def tiled(value, rows, lanes):
    if value.shape[0] != rows:
        value = jnp.concatenate([value] * (rows // value.shape[0]), axis=0)
    if value.shape[1] != lanes:
        value = jnp.concatenate([value] * (lanes // value.shape[1]), axis=1)
    return value


def pick_mask(column16, lane16):
    rows, lanes = (column16.shape[0], lane16.shape[1])
    same = tiled(column16, rows, lanes) == tiled(lane16, rows, lanes)
    return jnp.where(same, jnp.bfloat16(1), jnp.bfloat16(0))


def sum_mask(row, rows16, scale=None):
    count, length = (rows16.shape[0], row.shape[1])
    targets = jnp.broadcast_to(row, (16, length)).astype(jnp.int16)
    same = tiled(rows16, count, length) == tiled(targets, count, length)
    if scale is None:
        here = jnp.bfloat16(1)
    else:
        here = tiled(jnp.broadcast_to(scale, (16, length)).astype(jnp.bfloat16), count, length)
    return jnp.where(same, here, jnp.bfloat16(0))


def dot(a, b):
    return jnp.dot(a, b, preferred_element_type=jnp.float32)


def block_index(meets, reach):
    return reach if meets is None else block_for(meets, reach)


def pick_kernel(groups, index_ref, table_ref, *refs):
    out_refs = refs[-len(groups) :]
    lanes = lane_iota(table_ref.shape[0])
    reach = index_ref.shape[0] // 2
    for group, out_ref in zip(groups, out_refs):
        for place, meets in enumerate(group):
            col = column(index_ref[block_index(meets, reach)]).astype(jnp.int16)
            out_ref[place] = dot(pick_mask(col, lanes), table_ref[...]).astype(jnp.bfloat16)


def pick(groups, g2m_src, grid_latent, after=()):
    capacity = g2m_src.shape[2]
    rows, channels = grid_latent.shape
    return call(
        functools.partial(pick_kernel, groups),
        [shape((len(group), capacity, channels)) for group in groups],
        [g2m_src, grid_latent, *after],
        2 * sum(map(len, groups)) * capacity * rows * channels,
    )


def first_pick_kernel(groups, parts, index_hbm, table_hbm, *refs):
    out_refs, (index_ref, table_ref, index_sem, table_sems) = (refs[: len(groups)], refs[len(groups) :])
    rows = table_ref.shape[0] // parts
    index_copy = pltpu.make_async_copy(index_hbm, index_ref, index_sem)
    index_copy.start()
    copies = []
    for part in range(parts):
        here = pl.ds(part * rows, rows)
        copies.append(pltpu.make_async_copy(table_hbm.at[here, :], table_ref.at[here, :], table_sems.at[part]))
        copies[-1].start()
    index_copy.wait()
    reach = index_ref.shape[0] // 2
    cols = [
        column(index_ref[block_index(meets, reach)]).astype(jnp.int16) for group in groups for meets in group
    ]
    totals = [None] * len(cols)
    for part, copy in enumerate(copies):
        copy.wait()
        lanes = (lane_iota(rows).astype(jnp.int32) + part * rows).astype(jnp.int16)
        for k, col in enumerate(cols):
            found = dot(pick_mask(col, lanes), table_ref[pl.ds(part * rows, rows), :])
            totals[k] = found if part == 0 else totals[k] + found
    for group, out_ref in zip(groups, out_refs):
        for place in range(len(group)):
            out_ref[place] = totals.pop(0).astype(jnp.bfloat16)


def first_pick(groups, g2m_src, grid_latent):
    capacity = g2m_src.shape[2]
    rows, channels = grid_latent.shape
    parts = 4
    outputs = [shape((len(group), capacity, channels)) for group in groups]
    outputs += [shape(g2m_src.shape, g2m_src.dtype), shape(grid_latent.shape, grid_latent.dtype)]
    *picked, index, table = pl.pallas_call(
        functools.partial(first_pick_kernel, groups, parts),
        out_shape=[made_in_vmem(o) for o in outputs],
        in_specs=[pl.BlockSpec(memory_space=pl.ANY)] * 2,
        out_specs=[pl.BlockSpec(memory_space=pltpu.VMEM)] * len(outputs),
        scratch_shapes=[pltpu.SemaphoreType.DMA, pltpu.SemaphoreType.DMA((parts,))],
        compiler_params=pltpu.CompilerParams(vmem_limit_bytes=VMEM_BYTES),
    )(taken_from_hbm(g2m_src), taken_from_hbm(grid_latent))
    return picked, index, table


def fetch_kernel(after_ref, *refs):
    count = (len(refs) - 3) // 2
    sources, copied, (source_col_ref, target_col_ref, sems) = (
        refs[:count],
        refs[count : 2 * count],
        refs[2 * count :],
    )
    copies = [pltpu.make_async_copy(sources[k], copied[k], sems.at[k]) for k in range(count)]
    for copy in copies:
        copy.start()
    for copy, row_ref, out_ref in zip(copies, copied, (source_col_ref, target_col_ref)):
        copy.wait()
        out_ref[...] = column(row_ref[...]).astype(jnp.int16)
    for copy in copies[2:]:
        copy.wait()


def fetch(after, *arrays):
    outputs = [shape(a.shape, a.dtype) for a in arrays]
    outputs += [shape((a.shape[1], 128), jnp.int16) for a in arrays[:2]]
    return pl.pallas_call(
        fetch_kernel,
        out_shape=[made_in_vmem(o) for o in outputs],
        in_specs=[pl.BlockSpec(memory_space=pltpu.VMEM)] + [pl.BlockSpec(memory_space=pl.ANY)] * len(arrays),
        out_specs=[pl.BlockSpec(memory_space=pltpu.VMEM)] * len(outputs),
        scratch_shapes=[pltpu.SemaphoreType.DMA((len(arrays),))],
        compiler_params=pltpu.CompilerParams(vmem_limit_bytes=VMEM_BYTES),
    )(taken_from_vmem(after), *[taken_from_hbm(a) for a in arrays])


def encode_kernel(group, others, weight_ref, coef_ref, target_ref, *refs):
    sources, outs = (refs[: others + 1], refs[-len(group) :])
    capacity, channels = sources[0].shape[1:]
    weights = own_and_others_rows(weight_ref, channels, others)
    line = lax.broadcasted_iota(jnp.int32, (PAD, channels), 0)
    pieces = capacity // channels
    reach = coef_ref.shape[0] // 2
    for place, meets in enumerate(group):
        j = block_index(meets, reach)
        projected = dot(sources[0][place], weights[0])
        for source, weight in zip(sources[1:], weights[1:]):
            projected += dot(source[place], weight)
        scale = tiled(column(coef_ref[j]), capacity, channels)
        outs[place][pl.ds(0, capacity), :] = (scale * silu(projected)).astype(jnp.bfloat16)
        target = target_ref[j]
        code = jnp.zeros((PAD, channels), jnp.float32)
        for number, part in enumerate((target >> 3, target & 7)):
            part = part.astype(jnp.float32)
            for piece in range(pieces):
                values = part[:, piece * channels : (piece + 1) * channels]
                code = jnp.where(line == number * pieces + piece, values, code)
        outs[place][pl.ds(capacity, PAD), :] = code.astype(jnp.bfloat16)


def encode(group, picked, arrived, enc_weight, g2m_coef, g2m_dst, after=()):
    count, capacity, channels = picked.shape
    return call(
        functools.partial(encode_kernel, group, len(arrived)),
        [shape((capacity + PAD, channels))] * count,
        [enc_weight, g2m_coef, g2m_dst, picked, *arrived, *after],
        2 * count * capacity * enc_weight.shape[0] * channels,
        count * capacity * channels,
    )


def gather_in_kernel(before_ref, *refs):
    blocks, out_ref = (refs[:-1], refs[-1])
    nodes, channels = before_ref.shape
    capacity = blocks[0].shape[0] - PAD
    rows16 = row_iota(nodes)
    pieces = capacity // channels
    total = before_ref[...].astype(jnp.float32)
    for block in blocks:
        code = block[pl.ds(capacity, PAD), :].astype(jnp.float32)
        lines = [code[i : i + 1, :] for i in range(2 * pieces)]
        upper = lines[0] if pieces == 1 else jnp.concatenate(lines[:pieces], axis=1)
        lower = lines[1] if pieces == 1 else jnp.concatenate(lines[pieces:], axis=1)
        target = (8.0 * upper + lower).astype(jnp.int32)
        total += dot(sum_mask(target, rows16), block[pl.ds(0, capacity), :])
    out_ref[...] = total.astype(out_ref.dtype)


def gather_in(before, blocks, dtype):
    nodes, channels = before.shape
    slots = len(blocks) * blocks[0].shape[0]
    return call(
        gather_in_kernel,
        [shape((nodes, channels), dtype)],
        [before, *blocks],
        2 * nodes * slots * channels,
    )[0]


def list_kernel(reach, listed_ref, state_ref, far_ref, near_ref, one_ref, two_ref):
    nodes = state_ref.shape[0]
    width = listed_ref.shape[2]
    lanes = lane_iota(nodes)
    region = lax.axis_index(REGION)
    core = region % 2
    wanted = [
        meets(region) - core + i - region for meets in (meets_two, meets_other_two) for i in range(2)
    ]
    wanted += [meets_other_three(region) - region, meets_core(region) - region]
    wanted = [offset + reach - jnp.where(offset > 0, 1, 0) for offset in wanted]
    for k in range(0, len(wanted), 2):
        row = jnp.concatenate([listed_ref[wanted[k + i]] for i in range(2)], axis=1)
        rows = dot(pick_mask(column(row).astype(jnp.int16), lanes), state_ref[...])
        rows = rows.astype(jnp.bfloat16)
        parts = [rows[i * width : (i + 1) * width] for i in range(2)]
        if k < 4:
            ref = one_ref if k == 0 else two_ref
            for i in range(2):
                ref[i] = parts[i]
        else:
            far_ref[pl.ds(0, width), :] = parts[0]
            far_ref[pl.ds(width, far_ref.shape[0] - width), :] = jnp.zeros(
                (far_ref.shape[0] - width, parts[0].shape[1]), jnp.bfloat16
            )
            near_ref[...] = parts[1]


def list_rows(state, halo_send, reach):
    nodes, channels = state.shape
    links, unused, width = halo_send.shape
    one, two = [shape(d) for d in ((width, channels), (2, width, channels))]
    far = shape((2 * width + PAD, channels))
    return call(
        functools.partial(list_kernel, reach),
        [far, one, two, two],
        [halo_send, state],
        0,
    )


def forward_kernel(distant_ref, near_ref, one_ref, two_ref, sent_ref, mine_ref):
    width = near_ref.shape[0]
    core = lax.axis_index("edge")
    for k, part in enumerate((near_ref[...], one_ref[1 - core], two_ref[1 - core])):
        sent_ref[pl.ds(k * width, width), :] = part
    for k, part in enumerate((distant_ref[pl.ds(0, width), :], one_ref[core], two_ref[core])):
        mine_ref[pl.ds(k * width, width), :] = part


def exchange_listed(far, near, one, two):
    width, channels = near.shape
    distant = swapped(far, meets_other_three)
    one, two = swapped(one, meets_two), swapped(two, meets_other_two)
    half = shape((3 * width, channels))
    sent, mine = call(forward_kernel, [half, half], [distant, near, one, two], 0)
    across = swapped(sent, meets_core)
    return [mine, *from_others(mine)], [across, *from_others(across)]


def ordered_rows(direct, across):
    width = direct.shape[0] // 3
    region = lax.axis_index(REGION)
    even = region % 2 == 0
    low_even = region // 2 % 2 == 0
    distant, *own = [direct[k * width : (k + 1) * width] for k in range(3)]
    near, *crossed = [across[k * width : (k + 1) * width] for k in range(3)]
    before, after = [
        [jnp.where(low_even == first, pair[0], pair[1]) for pair in (own, crossed)] for first in (False, True)
    ]
    rows = (
        jnp.where(even, after[1], distant),
        after[0],
        jnp.where(even, near, after[1]),
        jnp.where(even, before[1], near),
        before[0],
        jnp.where(even, distant, before[1]),
    )
    return jnp.concatenate(rows, axis=0)


def projected_rows(weight_ref, parts):
    weights = own_and_others_rows(weight_ref, parts[0].shape[1], len(parts) - 1)
    total = dot(parts[0][...], weights[0])
    for part, weight in zip(parts[1:], weights[1:]):
        total += dot(part[...], weight)
    return total.astype(jnp.bfloat16)


def project_kernel(layer, src_ref, dst_ref, *refs):
    states, table_ref = (refs[:-1], refs[-1])
    nodes = states[0].shape[0]
    table_ref[pl.ds(0, nodes), :] = projected_rows(src_ref.at[layer], states)
    table_ref[pl.ds(nodes, nodes), :] = projected_rows(dst_ref.at[layer], states)


def project(layer, states, src_weights, dst_weights):
    nodes, channels = states[0].shape
    depth = src_weights.shape[1]
    return call(
        functools.partial(project_kernel, layer),
        [shape((2 * nodes, channels))],
        [src_weights, dst_weights, *states],
        4 * nodes * depth * channels,
    )[0]


def first_kernel(turn, source_ref, target_ref, table_ref, out_ref):
    lanes = lane_iota(table_ref.shape[0] // 2)
    for start in range(0, source_ref.shape[0], turn):
        here = pl.ds(start, turn)
        mask = jnp.concatenate(
            [pick_mask(source_ref[here, :], lanes), pick_mask(target_ref[here, :], lanes)], axis=1
        )
        out_ref[here, :] = dot(mask, table_ref[...])


def first_part(source_col, target_col, table):
    rows, channels = table.shape
    edges = source_col.shape[0]
    return call(
        functools.partial(first_kernel, 512),
        [shape((edges, channels), jnp.float32)],
        [source_col, target_col, table],
        2 * edges * rows * channels,
    )[0]


def message_kernel(
    turn, turns, layer, source_ref, target_ref, coef_ref, state_ref, first_ref, weight_ref, *refs
):
    listed, (out_ref, message_ref) = (refs[:-2], refs[-2:])
    nodes, channels = state_ref.shape
    half = len(listed) // 2
    table = ordered_rows(
        projected_rows(weight_ref.at[layer], listed[:half]), projected_rows(weight_ref.at[layer], listed[half:])
    )
    lanes = (lane_iota(table.shape[0]).astype(jnp.int32) + nodes).astype(jnp.int16)
    rows16 = row_iota(nodes)
    total = state_ref[...].astype(jnp.float32)
    edges = source_ref.shape[0]

    def gathered(start):
        here = pl.ds(start, turn)
        return first_ref[here, :] + dot(pick_mask(source_ref[here, :], lanes), table)

    ahead = gathered(0)
    for start in range(0, edges, turn):
        summed = ahead
        if start + turn < edges:
            ahead = gathered(start + turn)
        message_ref[pl.ds(start, turn), :] = silu(summed).astype(jnp.bfloat16)
        done = start // turn + 1
        if done % turns == 0:
            here = pl.ds((done - turns) * turn, turns * turn)
            mask = sum_mask(target_ref[:, here], rows16, coef_ref[:, here])
            total += dot(mask, message_ref[here, :])
    out_ref[...] = total.astype(jnp.bfloat16)


def messages(layer, source_col, m2m_dst, m2m_coef, state, first, src_weights, listed, final):
    nodes, channels = state.shape
    edges = m2m_dst.shape[1]
    named = 2 * listed[0].shape[0]
    return call(
        functools.partial(message_kernel, 512, 5, layer),
        [shape((nodes, channels))],
        [source_col, m2m_dst, m2m_coef, state, first, src_weights, *listed],
        2 * edges * (named + nodes) * channels,
        edges * channels,
        [pltpu.VMEM((edges, channels), jnp.bfloat16)],
        final,
    )[0]


def on_device(
    grid_latent,
    enc_weight,
    mesh_latent,
    g2m_src,
    g2m_dst,
    g2m_coef,
    src_weights,
    dst_weights,
    halo_send,
    m2m_src,
    m2m_dst,
    m2m_coef,
):
    reach = (g2m_src.shape[1] - 1) // 2
    assert reach == 3 and lax.axis_size("edge") == 2
    g2m_src, g2m_dst, g2m_coef, halo_send = [
        jnp.swapaxes(a, 0, 1) for a in (g2m_src, g2m_dst, g2m_coef, halo_send)
    ]
    groups = [
        (meets_other_three,), (meets_three,), (meets_two, meets_other_two), (meets_next, None), (meets_core,)
    ]
    picked, g2m_src, grid_latent = first_pick(groups[:2], g2m_src, grid_latent)
    arrived = [from_others(rows, group[0]) for group, rows in zip(groups, picked)]
    m2m_src, m2m_dst, m2m_coef, enc_weight, g2m_coef, g2m_dst, mesh_latent, halo_send, src_weights, dst_weights, *cols = (
        fetch(
            g2m_src, m2m_src, m2m_dst, m2m_coef, enc_weight, g2m_coef, g2m_dst, mesh_latent, halo_send,
            src_weights, dst_weights,
        )
    )
    source_col, target_col = cols

    def pick_next(place, after):
        picked.extend(pick(groups[place : place + 1], g2m_src, grid_latent, after))
        arrived.append(from_others(picked[place]))

    def encode_group(place, after=()):
        return encode(groups[place], picked[place], arrived[place], enc_weight, g2m_coef, g2m_dst, after)

    pick_next(2, [*arrived[0], source_col])
    pick_next(3, arrived[1])
    encoded = encode_group(0) + encode_group(1)
    encoded += encode_group(2)
    blocks = [swapped(block, meets) for block, meets in zip(encoded, groups[0] + groups[1] + groups[2])]
    state = gather_in(mesh_latent, blocks[:2], jnp.float32)
    pick_next(4, [state, *encoded[2:]])
    following, own = encode_group(3)
    (near,) = encode_group(4)
    blocks.append(swapped(following, meets_next))
    near = swapped(near, meets_core)
    state = gather_in(state, blocks[2:4] + [own], jnp.float32)
    state = gather_in(state, [blocks[4], near], jnp.bfloat16)
    layers = src_weights.shape[0]
    for layer in range(layers):
        others = from_others(state)
        direct, across = exchange_listed(*list_rows(state, halo_send, reach))
        table = project(layer, [state, *others], src_weights, dst_weights)
        first = first_part(source_col, target_col, table)
        state = messages(
            layer, source_col, m2m_dst, m2m_coef, state, first, src_weights, direct + across, layer == layers - 1
        )
    return state


def solution(mesh):
    placed = (
        P(("groups", "space", "edge"), "feat"),
        P(None, "feat"),
        P(("groups", "space", "edge"), "feat"),
        P(("groups", "space", "edge"), None, None),
        P(("groups", "space", "edge"), None, None),
        P(("groups", "space", "edge"), None, None),
        P(None, None, "feat"),
        P(None, None, "feat"),
        P(("groups", "space", "edge"), None, None),
        P(("groups", "space", "edge"), None),
        P(("groups", "space", "edge"), None),
        P(("groups", "space", "edge"), None),
    )
    return jax.shard_map(
        on_device,
        mesh=mesh,
        in_specs=placed,
        out_specs=P(("groups", "space", "edge"), "feat"),
        check_vma=False,
    )
```

```python
import functools

import jax
import jax.numpy as jnp
from jax import lax
from jax.experimental import pallas as pl
from jax.experimental.pallas import tpu as pltpu
from jax.sharding import PartitionSpec as P

REGION = ("space", "edge")
PAD = 16
VMEM_BYTES = 28 * 1024 * 1024


def made_in_vmem(output):
    return pltpu.VMEM(output.shape, output.dtype)


def taken_from_vmem(array):
    return pltpu.with_memory_space_constraint(array, pltpu.VMEM)


def taken_from_hbm(array):
    return pltpu.with_memory_space_constraint(array, pltpu.HBM)


def call(kernel, outputs, inputs, flops, transcendentals=0, scratch=(), final=False, fetched=0):
    size = lambda a: int(a.size) * a.dtype.itemsize
    shapes = outputs if final else [made_in_vmem(o) for o in outputs]
    return pl.pallas_call(
        kernel,
        out_shape=shapes,
        in_specs=[pl.BlockSpec(memory_space=pltpu.VMEM)] * len(inputs),
        out_specs=[pl.BlockSpec(memory_space=pltpu.VMEM)] * len(outputs),
        scratch_shapes=list(scratch),
        compiler_params=pltpu.CompilerParams(vmem_limit_bytes=VMEM_BYTES),
        cost_estimate=pl.CostEstimate(
            flops=flops,
            bytes_accessed=sum(size(a) for a in list(inputs) + list(outputs)) if flops else 0,
            transcendentals=transcendentals,
        ),
    )(*inputs[:fetched], *[taken_from_vmem(a) for a in inputs[fetched:]])


def shape(dims, dtype=jnp.bfloat16):
    return jax.ShapeDtypeStruct(dims, dtype)


def meets_core(r):
    return r + 1 - 2 * (r % 2)


def meets_next(r):
    return r - 1 + 2 * (r % 2)


def meets_two(r):
    return r + 2 - 4 * (r // 2 % 2)


def meets_other_two(r):
    return r - 2 + 4 * (r // 2 % 2)


def meets_three(r):
    return r + 3 - 6 * (r % 2)


def meets_other_three(r):
    return r - 3 + 6 * (r % 2)


def pairs(meets):
    count = lax.axis_size(REGION)
    return [(r, meets(r)) for r in range(count) if 0 <= meets(r) < count]


def swapped(value, meets):
    return lax.ppermute(value, REGION, pairs(meets))


def block_for(meets, reach):
    region = lax.axis_index(REGION)
    return meets(region) - region + reach


def from_others(value, meets=None):
    n = lax.axis_size("feat")
    if meets is None:
        axes, rings = ("feat", [[i for i in range(n)]])
    else:
        axes, cores = (("space", "feat", "edge"), lax.axis_size("edge"))
        rings = [
            [(r // cores * n + i) * cores + r % cores for i in range(n)] for r, unused in pairs(meets)
        ]
    return [
        lax.ppermute(value, axes, [(ring[i], ring[(i + k) % n]) for ring in rings for i in range(n)])
        for k in range(1, n)
    ]


def own_and_others_rows(weight_ref, channels, others):
    n = others + 1
    me = lax.axis_index("feat")
    blocks = []
    for k in range(n):
        owner = lax.rem(me - k + n, n)
        start = pl.multiple_of(owner * channels, channels)
        blocks.append(weight_ref[pl.ds(start, channels), :])
    return blocks


def silu(v):
    half = 0.5 * v
    return half + half * jnp.tanh(half)


def column(row):
    length = row.shape[1]
    parts = [
        jnp.broadcast_to(row[:, c * 128 : (c + 1) * 128], (128, 128)).T for c in range(length // 128)
    ]
    return parts[0] if len(parts) == 1 else jnp.concatenate(parts, axis=0)


def lane_iota(count):
    return lax.broadcasted_iota(jnp.int32, (16, count), 1).astype(jnp.int16)


def row_iota(count):
    return lax.broadcasted_iota(jnp.int32, (count, 128), 0).astype(jnp.int16)


def tiled(value, rows, lanes):
    if value.shape[0] != rows:
        value = jnp.concatenate([value] * (rows // value.shape[0]), axis=0)
    if value.shape[1] != lanes:
        value = jnp.concatenate([value] * (lanes // value.shape[1]), axis=1)
    return value


def pick_mask(column16, lane16):
    rows, lanes = (column16.shape[0], lane16.shape[1])
    same = tiled(column16, rows, lanes) == tiled(lane16, rows, lanes)
    return jnp.where(same, jnp.bfloat16(1), jnp.bfloat16(0))


def sum_mask(row, rows16, scale=None):
    count, length = (rows16.shape[0], row.shape[1])
    targets = jnp.broadcast_to(row, (16, length)).astype(jnp.int16)
    same = tiled(rows16, count, length) == tiled(targets, count, length)
    if scale is None:
        here = jnp.bfloat16(1)
    else:
        here = tiled(jnp.broadcast_to(scale, (16, length)).astype(jnp.bfloat16), count, length)
    return jnp.where(same, here, jnp.bfloat16(0))


def dot(a, b):
    return jnp.dot(a, b, preferred_element_type=jnp.float32)


def block_index(meets, reach):
    return reach if meets is None else block_for(meets, reach)


def pick_kernel(groups, index_ref, table_ref, *refs):
    out_refs = refs[-len(groups) :]
    lanes = lane_iota(table_ref.shape[0])
    reach = index_ref.shape[0] // 2
    for group, out_ref in zip(groups, out_refs):
        for place, meets in enumerate(group):
            col = column(index_ref[block_index(meets, reach)]).astype(jnp.int16)
            out_ref[place] = dot(pick_mask(col, lanes), table_ref[...]).astype(jnp.bfloat16)


def pick(groups, g2m_src, grid_latent, after=()):
    capacity = g2m_src.shape[2]
    rows, channels = grid_latent.shape
    return call(
        functools.partial(pick_kernel, groups),
        [shape((len(group), capacity, channels)) for group in groups],
        [g2m_src, grid_latent, *after],
        2 * sum(map(len, groups)) * capacity * rows * channels,
    )


def first_pick_kernel(groups, parts, index_hbm, table_hbm, *refs):
    out_refs, (index_ref, table_ref, index_sem, table_sems) = (refs[: len(groups)], refs[len(groups) :])
    rows = table_ref.shape[0] // parts
    index_copy = pltpu.make_async_copy(index_hbm, index_ref, index_sem)
    index_copy.start()
    copies = []
    for part in range(parts):
        here = pl.ds(part * rows, rows)
        copies.append(pltpu.make_async_copy(table_hbm.at[here, :], table_ref.at[here, :], table_sems.at[part]))
        copies[-1].start()
    index_copy.wait()
    reach = index_ref.shape[0] // 2
    cols = [
        column(index_ref[block_index(meets, reach)]).astype(jnp.int16) for group in groups for meets in group
    ]
    totals = [None] * len(cols)
    for part, copy in enumerate(copies):
        copy.wait()
        lanes = (lane_iota(rows).astype(jnp.int32) + part * rows).astype(jnp.int16)
        for k, col in enumerate(cols):
            found = dot(pick_mask(col, lanes), table_ref[pl.ds(part * rows, rows), :])
            totals[k] = found if part == 0 else totals[k] + found
    for group, out_ref in zip(groups, out_refs):
        for place in range(len(group)):
            out_ref[place] = totals.pop(0).astype(jnp.bfloat16)


def first_pick(groups, g2m_src, grid_latent):
    capacity = g2m_src.shape[2]
    rows, channels = grid_latent.shape
    parts = 4
    outputs = [shape((len(group), capacity, channels)) for group in groups]
    outputs += [shape(g2m_src.shape, g2m_src.dtype), shape(grid_latent.shape, grid_latent.dtype)]
    *picked, index, table = pl.pallas_call(
        functools.partial(first_pick_kernel, groups, parts),
        out_shape=[made_in_vmem(o) for o in outputs],
        in_specs=[pl.BlockSpec(memory_space=pl.ANY)] * 2,
        out_specs=[pl.BlockSpec(memory_space=pltpu.VMEM)] * len(outputs),
        scratch_shapes=[pltpu.SemaphoreType.DMA, pltpu.SemaphoreType.DMA((parts,))],
        compiler_params=pltpu.CompilerParams(vmem_limit_bytes=VMEM_BYTES),
    )(taken_from_hbm(g2m_src), taken_from_hbm(grid_latent))
    return picked, index, table


def fetch_kernel(after_ref, *refs):
    count = (len(refs) - 1) // 2
    sources, copied, sems = (refs[:count], refs[count : 2 * count], refs[-1])
    copies = [pltpu.make_async_copy(sources[k], copied[k], sems.at[k]) for k in range(count)]
    for copy in copies:
        copy.start()
    for copy in copies:
        copy.wait()


def fetch(after, *arrays):
    outputs = [shape(a.shape, a.dtype) for a in arrays]
    return pl.pallas_call(
        fetch_kernel,
        out_shape=[made_in_vmem(o) for o in outputs],
        in_specs=[pl.BlockSpec(memory_space=pltpu.VMEM)] + [pl.BlockSpec(memory_space=pl.ANY)] * len(arrays),
        out_specs=[pl.BlockSpec(memory_space=pltpu.VMEM)] * len(outputs),
        scratch_shapes=[pltpu.SemaphoreType.DMA((len(arrays),))],
        compiler_params=pltpu.CompilerParams(vmem_limit_bytes=VMEM_BYTES),
    )(taken_from_vmem(after), *[taken_from_hbm(a) for a in arrays])


def columns_kernel(*refs):
    half = len(refs) // 2
    for row_ref, out_ref in zip(refs[:half], refs[half:]):
        out_ref[...] = column(row_ref[...]).astype(jnp.int16)


def columns(*rows):
    count = rows[0].shape[1]
    return call(
        columns_kernel, [shape((count, 128), jnp.int16)] * len(rows), rows, len(rows) * count * 128 * 8
    )


def encode_kernel(group, others, weight_ref, coef_ref, target_ref, *refs):
    sources, outs = (refs[: others + 1], refs[-len(group) :])
    capacity, channels = sources[0].shape[1:]
    weights = own_and_others_rows(weight_ref, channels, others)
    line = lax.broadcasted_iota(jnp.int32, (PAD, channels), 0)
    pieces = capacity // channels
    reach = coef_ref.shape[0] // 2
    for place, meets in enumerate(group):
        j = block_index(meets, reach)
        projected = dot(sources[0][place], weights[0])
        for source, weight in zip(sources[1:], weights[1:]):
            projected += dot(source[place], weight)
        scale = tiled(column(coef_ref[j]), capacity, channels)
        outs[place][pl.ds(0, capacity), :] = (scale * silu(projected)).astype(jnp.bfloat16)
        target = target_ref[j]
        code = jnp.zeros((PAD, channels), jnp.float32)
        for number, part in enumerate((target >> 3, target & 7)):
            part = part.astype(jnp.float32)
            for piece in range(pieces):
                values = part[:, piece * channels : (piece + 1) * channels]
                code = jnp.where(line == number * pieces + piece, values, code)
        outs[place][pl.ds(capacity, PAD), :] = code.astype(jnp.bfloat16)


def encode(group, picked, arrived, enc_weight, g2m_coef, g2m_dst, after=()):
    count, capacity, channels = picked.shape
    return call(
        functools.partial(encode_kernel, group, len(arrived)),
        [shape((capacity + PAD, channels))] * count,
        [enc_weight, g2m_coef, g2m_dst, picked, *arrived, *after],
        2 * count * capacity * enc_weight.shape[0] * channels,
        count * capacity * channels,
    )


def gather_in_kernel(count, before_ref, *refs):
    blocks, out_ref = (refs[:count], refs[-1])
    nodes, channels = before_ref.shape
    capacity = blocks[0].shape[0] - PAD
    rows16 = row_iota(nodes)
    pieces = capacity // channels
    total = before_ref[...].astype(jnp.float32)
    for block in blocks:
        code = block[pl.ds(capacity, PAD), :].astype(jnp.float32)
        lines = [code[i : i + 1, :] for i in range(2 * pieces)]
        upper = lines[0] if pieces == 1 else jnp.concatenate(lines[:pieces], axis=1)
        lower = lines[1] if pieces == 1 else jnp.concatenate(lines[pieces:], axis=1)
        target = (8.0 * upper + lower).astype(jnp.int32)
        total += dot(sum_mask(target, rows16), block[pl.ds(0, capacity), :])
    out_ref[...] = total.astype(out_ref.dtype)


def gather_in(before, blocks, dtype, after=()):
    nodes, channels = before.shape
    slots = len(blocks) * blocks[0].shape[0]
    return call(
        functools.partial(gather_in_kernel, len(blocks)),
        [shape((nodes, channels), dtype)],
        [before, *blocks, *after],
        2 * nodes * slots * channels,
    )[0]


def list_kernel(reach, listed_ref, state_ref, far_ref, near_ref, one_ref, two_ref):
    nodes = state_ref.shape[0]
    width = listed_ref.shape[2]
    lanes = lane_iota(nodes)
    region = lax.axis_index(REGION)
    core = region % 2
    wanted = [
        meets(region) - core + i - region for meets in (meets_two, meets_other_two) for i in range(2)
    ]
    wanted += [meets_other_three(region) - region, meets_core(region) - region]
    wanted = [offset + reach - jnp.where(offset > 0, 1, 0) for offset in wanted]
    for k in range(0, len(wanted), 2):
        row = jnp.concatenate([listed_ref[wanted[k + i]] for i in range(2)], axis=1)
        rows = dot(pick_mask(column(row).astype(jnp.int16), lanes), state_ref[...])
        rows = rows.astype(jnp.bfloat16)
        parts = [rows[i * width : (i + 1) * width] for i in range(2)]
        if k < 4:
            ref = one_ref if k == 0 else two_ref
            for i in range(2):
                ref[i] = parts[i]
        else:
            far_ref[pl.ds(0, width), :] = parts[0]
            far_ref[pl.ds(width, far_ref.shape[0] - width), :] = jnp.zeros(
                (far_ref.shape[0] - width, parts[0].shape[1]), jnp.bfloat16
            )
            near_ref[...] = parts[1]


def list_rows(state, halo_send, reach):
    nodes, channels = state.shape
    links, unused, width = halo_send.shape
    one, two = [shape(d) for d in ((width, channels), (2, width, channels))]
    far = shape((2 * width + PAD, channels))
    return call(
        functools.partial(list_kernel, reach),
        [far, one, two, two],
        [halo_send, state],
        0,
    )


def forward_kernel(distant_ref, near_ref, one_ref, two_ref, sent_ref, mine_ref):
    width = near_ref.shape[0]
    core = lax.axis_index("edge")
    for k, part in enumerate((near_ref[...], one_ref[1 - core], two_ref[1 - core])):
        sent_ref[pl.ds(k * width, width), :] = part
    for k, part in enumerate((distant_ref[pl.ds(0, width), :], one_ref[core], two_ref[core])):
        mine_ref[pl.ds(k * width, width), :] = part


def exchange_listed(far, near, one, two):
    width, channels = near.shape
    distant = swapped(far, meets_other_three)
    one, two = swapped(one, meets_two), swapped(two, meets_other_two)
    half = shape((3 * width, channels))
    sent, mine = call(forward_kernel, [half, half], [distant, near, one, two], 0)
    across = swapped(sent, meets_core)
    return [mine, *from_others(mine)], [across, *from_others(across)]


def ordered_rows(direct, across):
    width = direct.shape[0] // 3
    region = lax.axis_index(REGION)
    even = region % 2 == 0
    low_even = region // 2 % 2 == 0
    distant, *own = [direct[k * width : (k + 1) * width] for k in range(3)]
    near, *crossed = [across[k * width : (k + 1) * width] for k in range(3)]
    before, after = [
        [jnp.where(low_even == first, pair[0], pair[1]) for pair in (own, crossed)] for first in (False, True)
    ]
    rows = (
        jnp.where(even, after[1], distant),
        after[0],
        jnp.where(even, near, after[1]),
        jnp.where(even, before[1], near),
        before[0],
        jnp.where(even, distant, before[1]),
    )
    return jnp.concatenate(rows, axis=0)


def projected_rows(weight_ref, parts):
    weights = own_and_others_rows(weight_ref, parts[0].shape[1], len(parts) - 1)
    total = dot(parts[0][...], weights[0])
    for part, weight in zip(parts[1:], weights[1:]):
        total += dot(part[...], weight)
    return total.astype(jnp.bfloat16)


def project_kernel(layer, src_ref, dst_ref, *refs):
    states, table_ref = (refs[:-1], refs[-1])
    nodes = states[0].shape[0]
    table_ref[pl.ds(0, nodes), :] = projected_rows(src_ref.at[layer], states)
    table_ref[pl.ds(nodes, nodes), :] = projected_rows(dst_ref.at[layer], states)


def project(layer, states, src_weights, dst_weights):
    nodes, channels = states[0].shape
    depth = src_weights.shape[1]
    return call(
        functools.partial(project_kernel, layer),
        [shape((2 * nodes, channels))],
        [src_weights, dst_weights, *states],
        4 * nodes * depth * channels,
    )[0]


def first_kernel(turn, source_ref, target_ref, table_ref, out_ref):
    lanes = lane_iota(table_ref.shape[0] // 2)
    for start in range(0, source_ref.shape[0], turn):
        here = pl.ds(start, turn)
        mask = jnp.concatenate(
            [pick_mask(source_ref[here, :], lanes), pick_mask(target_ref[here, :], lanes)], axis=1
        )
        out_ref[here, :] = dot(mask, table_ref[...])


def first_part(source_col, target_col, table):
    rows, channels = table.shape
    edges = source_col.shape[0]
    return call(
        functools.partial(first_kernel, 512),
        [shape((edges, channels), jnp.float32)],
        [source_col, target_col, table],
        2 * edges * rows * channels,
    )[0]


def message_kernel(
    turn, turns, layer, source_ref, target_ref, coef_ref, state_ref, first_ref, weight_ref, *refs
):
    listed, (out_ref, message_ref) = (refs[:-2], refs[-2:])
    nodes, channels = state_ref.shape
    half = len(listed) // 2
    table = ordered_rows(
        projected_rows(weight_ref.at[layer], listed[:half]), projected_rows(weight_ref.at[layer], listed[half:])
    )
    lanes = (lane_iota(table.shape[0]).astype(jnp.int32) + nodes).astype(jnp.int16)
    rows16 = row_iota(nodes)
    total = state_ref[...].astype(jnp.float32)
    edges = source_ref.shape[0]

    def gathered(start):
        here = pl.ds(start, turn)
        return first_ref[here, :] + dot(pick_mask(source_ref[here, :], lanes), table)

    ahead = gathered(0)
    for start in range(0, edges, turn):
        summed = ahead
        if start + turn < edges:
            ahead = gathered(start + turn)
        message_ref[pl.ds(start, turn), :] = silu(summed).astype(jnp.bfloat16)
        done = start // turn + 1
        if done % turns == 0:
            here = pl.ds((done - turns) * turn, turns * turn)
            mask = sum_mask(target_ref[:, here], rows16, coef_ref[:, here])
            total += dot(mask, message_ref[here, :])
    out_ref[...] = total.astype(jnp.bfloat16)


def messages(layer, source_col, m2m_dst, m2m_coef, state, first, src_weights, listed, final):
    nodes, channels = state.shape
    edges = m2m_dst.shape[1]
    named = 2 * listed[0].shape[0]
    return call(
        functools.partial(message_kernel, 512, 5, layer),
        [shape((nodes, channels))],
        [source_col, m2m_dst, m2m_coef, state, first, src_weights, *listed],
        2 * edges * (named + nodes) * channels,
        edges * channels,
        [pltpu.VMEM((edges, channels), jnp.bfloat16)],
        final,
    )[0]


def on_device(
    grid_latent,
    enc_weight,
    mesh_latent,
    g2m_src,
    g2m_dst,
    g2m_coef,
    src_weights,
    dst_weights,
    halo_send,
    m2m_src,
    m2m_dst,
    m2m_coef,
):
    reach = (g2m_src.shape[1] - 1) // 2
    assert reach == 3 and lax.axis_size("edge") == 2
    g2m_src, g2m_dst, g2m_coef, halo_send = [
        jnp.swapaxes(a, 0, 1) for a in (g2m_src, g2m_dst, g2m_coef, halo_send)
    ]
    groups = [
        (meets_other_three,), (meets_three,), (meets_two, meets_other_two), (meets_next, None), (meets_core,)
    ]
    picked, g2m_src, grid_latent = first_pick(groups[:2], g2m_src, grid_latent)
    arrived = [from_others(rows, group[0]) for group, rows in zip(groups, picked)]
    m2m_src, m2m_dst, m2m_coef, enc_weight, g2m_coef, g2m_dst, mesh_latent, halo_send, src_weights, dst_weights = (
        fetch(
            g2m_src, m2m_src, m2m_dst, m2m_coef, enc_weight, g2m_coef, g2m_dst, mesh_latent, halo_send,
            src_weights, dst_weights,
        )
    )
    source_col, target_col = cols = columns(m2m_src, m2m_dst)

    def pick_next(place, after):
        picked.extend(pick(groups[place : place + 1], g2m_src, grid_latent, after))
        arrived.append(from_others(picked[place]))

    def encode_group(place, after=()):
        return encode(groups[place], picked[place], arrived[place], enc_weight, g2m_coef, g2m_dst, after)

    pick_next(2, [*arrived[0], enc_weight])
    encoded = encode_group(0) + encode_group(1)
    pick_next(3, encoded)
    encoded += encode_group(2)
    blocks = [swapped(block, meets) for block, meets in zip(encoded, groups[0] + groups[1] + groups[2])]
    far_sum = gather_in(mesh_latent, blocks[:1], jnp.float32)
    state = gather_in(far_sum, blocks[1:2], jnp.float32)
    pick_next(4, [far_sum, *encoded[2:]])
    following, own = encode_group(3, [state])
    (near,) = encode_group(4)
    blocks.append(swapped(following, meets_next))
    near = swapped(near, meets_core)
    state = gather_in(state, blocks[2:4] + [own], jnp.float32, cols)
    state = gather_in(state, [blocks[4], near], jnp.bfloat16)
    layers = src_weights.shape[0]
    for layer in range(layers):
        others = from_others(state)
        direct, across = exchange_listed(*list_rows(state, halo_send, reach))
        table = project(layer, [state, *others], src_weights, dst_weights)
        first = first_part(source_col, target_col, table)
        state = messages(
            layer, source_col, m2m_dst, m2m_coef, state, first, src_weights, direct + across, layer == layers - 1
        )
    return state


def solution(mesh):
    placed = (
        P(("groups", "space", "edge"), "feat"),
        P(None, "feat"),
        P(("groups", "space", "edge"), "feat"),
        P(("groups", "space", "edge"), None, None),
        P(("groups", "space", "edge"), None, None),
        P(("groups", "space", "edge"), None, None),
        P(None, None, "feat"),
        P(None, None, "feat"),
        P(("groups", "space", "edge"), None, None),
        P(("groups", "space", "edge"), None),
        P(("groups", "space", "edge"), None),
        P(("groups", "space", "edge"), None),
    )
    return jax.shard_map(
        on_device,
        mesh=mesh,
        in_specs=placed,
        out_specs=P(("groups", "space", "edge"), "feat"),
        check_vma=False,
    )
```

```python
import functools

import jax
import jax.numpy as jnp
from jax import lax
from jax.experimental import pallas as pl
from jax.experimental.pallas import tpu as pltpu
from jax.sharding import PartitionSpec as P

REGION = ("space", "edge")
PAD = 16
VMEM_BYTES = 28 * 1024 * 1024


def made_in_vmem(output):
    return pltpu.VMEM(output.shape, output.dtype)


def taken_from_vmem(array):
    return pltpu.with_memory_space_constraint(array, pltpu.VMEM)


def taken_from_hbm(array):
    return pltpu.with_memory_space_constraint(array, pltpu.HBM)


def call(kernel, outputs, inputs, flops, transcendentals=0, scratch=(), final=False, fetched=0):
    size = lambda a: int(a.size) * a.dtype.itemsize
    shapes = outputs if final else [made_in_vmem(o) for o in outputs]
    return pl.pallas_call(
        kernel,
        out_shape=shapes,
        in_specs=[pl.BlockSpec(memory_space=pltpu.VMEM)] * len(inputs),
        out_specs=[pl.BlockSpec(memory_space=pltpu.VMEM)] * len(outputs),
        scratch_shapes=list(scratch),
        compiler_params=pltpu.CompilerParams(vmem_limit_bytes=VMEM_BYTES),
        cost_estimate=pl.CostEstimate(
            flops=flops,
            bytes_accessed=sum(size(a) for a in list(inputs) + list(outputs)) if flops else 0,
            transcendentals=transcendentals,
        ),
    )(*inputs[:fetched], *[taken_from_vmem(a) for a in inputs[fetched:]])


def shape(dims, dtype=jnp.bfloat16):
    return jax.ShapeDtypeStruct(dims, dtype)


def meets_core(r):
    return r + 1 - 2 * (r % 2)


def meets_next(r):
    return r - 1 + 2 * (r % 2)


def meets_two(r):
    return r + 2 - 4 * (r // 2 % 2)


def meets_other_two(r):
    return r - 2 + 4 * (r // 2 % 2)


def meets_three(r):
    return r + 3 - 6 * (r % 2)


def meets_other_three(r):
    return r - 3 + 6 * (r % 2)


def pairs(meets):
    count = lax.axis_size(REGION)
    return [(r, meets(r)) for r in range(count) if 0 <= meets(r) < count]


def swapped(value, meets):
    return lax.ppermute(value, REGION, pairs(meets))


def block_for(meets, reach):
    region = lax.axis_index(REGION)
    return meets(region) - region + reach


def from_others(value, meets=None):
    n = lax.axis_size("feat")
    if meets is None:
        axes, rings = ("feat", [[i for i in range(n)]])
    else:
        axes, cores = (("space", "feat", "edge"), lax.axis_size("edge"))
        rings = [
            [(r // cores * n + i) * cores + r % cores for i in range(n)] for r, unused in pairs(meets)
        ]
    return [
        lax.ppermute(value, axes, [(ring[i], ring[(i + k) % n]) for ring in rings for i in range(n)])
        for k in range(1, n)
    ]


def own_and_others_rows(weight_ref, channels, others):
    n = others + 1
    me = lax.axis_index("feat")
    blocks = []
    for k in range(n):
        owner = lax.rem(me - k + n, n)
        start = pl.multiple_of(owner * channels, channels)
        blocks.append(weight_ref[pl.ds(start, channels), :])
    return blocks


def silu(v):
    half = 0.5 * v
    return half + half * jnp.tanh(half)


def column(row):
    length = row.shape[1]
    parts = [
        jnp.broadcast_to(row[:, c * 128 : (c + 1) * 128], (128, 128)).T for c in range(length // 128)
    ]
    return parts[0] if len(parts) == 1 else jnp.concatenate(parts, axis=0)


def lane_iota(count):
    return lax.broadcasted_iota(jnp.int32, (16, count), 1).astype(jnp.int16)


def row_iota(count):
    return lax.broadcasted_iota(jnp.int32, (count, 128), 0).astype(jnp.int16)


def tiled(value, rows, lanes):
    if value.shape[0] != rows:
        value = jnp.concatenate([value] * (rows // value.shape[0]), axis=0)
    if value.shape[1] != lanes:
        value = jnp.concatenate([value] * (lanes // value.shape[1]), axis=1)
    return value


def pick_mask(column16, lane16):
    rows, lanes = (column16.shape[0], lane16.shape[1])
    same = tiled(column16, rows, lanes) == tiled(lane16, rows, lanes)
    return jnp.where(same, jnp.bfloat16(1), jnp.bfloat16(0))


def sum_mask(row, rows16, scale=None):
    count, length = (rows16.shape[0], row.shape[1])
    targets = jnp.broadcast_to(row, (16, length)).astype(jnp.int16)
    same = tiled(rows16, count, length) == tiled(targets, count, length)
    if scale is None:
        here = jnp.bfloat16(1)
    else:
        here = tiled(jnp.broadcast_to(scale, (16, length)).astype(jnp.bfloat16), count, length)
    return jnp.where(same, here, jnp.bfloat16(0))


def dot(a, b):
    return jnp.dot(a, b, preferred_element_type=jnp.float32)


def block_index(meets, reach):
    return reach if meets is None else block_for(meets, reach)


def pick_kernel(groups, index_ref, table_ref, *refs):
    out_refs = refs[-len(groups) :]
    lanes = lane_iota(table_ref.shape[0])
    reach = index_ref.shape[0] // 2
    for group, out_ref in zip(groups, out_refs):
        for place, meets in enumerate(group):
            col = column(index_ref[block_index(meets, reach)]).astype(jnp.int16)
            out_ref[place] = dot(pick_mask(col, lanes), table_ref[...]).astype(jnp.bfloat16)


def pick(groups, g2m_src, grid_latent, after=()):
    capacity = g2m_src.shape[2]
    rows, channels = grid_latent.shape
    return call(
        functools.partial(pick_kernel, groups),
        [shape((len(group), capacity, channels)) for group in groups],
        [g2m_src, grid_latent, *after],
        2 * sum(map(len, groups)) * capacity * rows * channels,
    )


def first_pick_kernel(groups, parts, index_hbm, table_hbm, *refs):
    out_refs, (index_ref, table_ref, index_sem, table_sems) = (refs[: len(groups)], refs[len(groups) :])
    rows = table_ref.shape[0] // parts
    index_copy = pltpu.make_async_copy(index_hbm, index_ref, index_sem)
    index_copy.start()
    copies = []
    for part in range(parts):
        here = pl.ds(part * rows, rows)
        copies.append(pltpu.make_async_copy(table_hbm.at[here, :], table_ref.at[here, :], table_sems.at[part]))
        copies[-1].start()
    index_copy.wait()
    reach = index_ref.shape[0] // 2
    cols = [
        column(index_ref[block_index(meets, reach)]).astype(jnp.int16) for group in groups for meets in group
    ]
    totals = [None] * len(cols)
    for part, copy in enumerate(copies):
        copy.wait()
        lanes = (lane_iota(rows).astype(jnp.int32) + part * rows).astype(jnp.int16)
        for k, col in enumerate(cols):
            found = dot(pick_mask(col, lanes), table_ref[pl.ds(part * rows, rows), :])
            totals[k] = found if part == 0 else totals[k] + found
    for group, out_ref in zip(groups, out_refs):
        for place in range(len(group)):
            out_ref[place] = totals.pop(0).astype(jnp.bfloat16)


def first_pick(groups, g2m_src, grid_latent):
    capacity = g2m_src.shape[2]
    rows, channels = grid_latent.shape
    parts = 4
    outputs = [shape((len(group), capacity, channels)) for group in groups]
    outputs += [shape(g2m_src.shape, g2m_src.dtype), shape(grid_latent.shape, grid_latent.dtype)]
    *picked, index, table = pl.pallas_call(
        functools.partial(first_pick_kernel, groups, parts),
        out_shape=[made_in_vmem(o) for o in outputs],
        in_specs=[pl.BlockSpec(memory_space=pl.ANY)] * 2,
        out_specs=[pl.BlockSpec(memory_space=pltpu.VMEM)] * len(outputs),
        scratch_shapes=[pltpu.SemaphoreType.DMA, pltpu.SemaphoreType.DMA((parts,))],
        compiler_params=pltpu.CompilerParams(vmem_limit_bytes=VMEM_BYTES),
    )(taken_from_hbm(g2m_src), taken_from_hbm(grid_latent))
    return picked, index, table


def fetch_kernel(after_ref, *refs):
    count = (len(refs) - 1) // 2
    sources, copied, sems = (refs[:count], refs[count : 2 * count], refs[-1])
    copies = [pltpu.make_async_copy(sources[k], copied[k], sems.at[k]) for k in range(count)]
    for copy in copies:
        copy.start()
    for copy in copies:
        copy.wait()


def fetch(after, *arrays):
    outputs = [shape(a.shape, a.dtype) for a in arrays]
    return pl.pallas_call(
        fetch_kernel,
        out_shape=[made_in_vmem(o) for o in outputs],
        in_specs=[pl.BlockSpec(memory_space=pltpu.VMEM)] + [pl.BlockSpec(memory_space=pl.ANY)] * len(arrays),
        out_specs=[pl.BlockSpec(memory_space=pltpu.VMEM)] * len(outputs),
        scratch_shapes=[pltpu.SemaphoreType.DMA((len(arrays),))],
        compiler_params=pltpu.CompilerParams(vmem_limit_bytes=VMEM_BYTES),
    )(taken_from_vmem(after), *[taken_from_hbm(a) for a in arrays])


def columns_kernel(*refs):
    half = len(refs) // 2
    for row_ref, out_ref in zip(refs[:half], refs[half:]):
        out_ref[...] = column(row_ref[...]).astype(jnp.int16)


def columns(*rows):
    count = rows[0].shape[1]
    return call(
        columns_kernel, [shape((count, 128), jnp.int16)] * len(rows), rows, len(rows) * count * 128 * 8
    )


def encode_kernel(group, others, weight_ref, coef_ref, target_ref, *refs):
    sources, outs = (refs[: others + 1], refs[-len(group) :])
    capacity, channels = sources[0].shape[1:]
    weights = own_and_others_rows(weight_ref, channels, others)
    line = lax.broadcasted_iota(jnp.int32, (PAD, channels), 0)
    pieces = capacity // channels
    reach = coef_ref.shape[0] // 2
    for place, meets in enumerate(group):
        j = block_index(meets, reach)
        projected = dot(sources[0][place], weights[0])
        for source, weight in zip(sources[1:], weights[1:]):
            projected += dot(source[place], weight)
        scale = tiled(column(coef_ref[j]), capacity, channels)
        outs[place][pl.ds(0, capacity), :] = (scale * silu(projected)).astype(jnp.bfloat16)
        target = target_ref[j]
        code = jnp.zeros((PAD, channels), jnp.float32)
        for number, part in enumerate((target >> 3, target & 7)):
            part = part.astype(jnp.float32)
            for piece in range(pieces):
                values = part[:, piece * channels : (piece + 1) * channels]
                code = jnp.where(line == number * pieces + piece, values, code)
        outs[place][pl.ds(capacity, PAD), :] = code.astype(jnp.bfloat16)


def encode(group, picked, arrived, enc_weight, g2m_coef, g2m_dst, after=()):
    count, capacity, channels = picked.shape
    return call(
        functools.partial(encode_kernel, group, len(arrived)),
        [shape((capacity + PAD, channels))] * count,
        [enc_weight, g2m_coef, g2m_dst, picked, *arrived, *after],
        2 * count * capacity * enc_weight.shape[0] * channels,
        count * capacity * channels,
    )


def gather_in_kernel(count, before_ref, *refs):
    blocks, out_ref = (refs[:count], refs[-1])
    nodes, channels = before_ref.shape
    capacity = blocks[0].shape[0] - PAD
    rows16 = row_iota(nodes)
    pieces = capacity // channels
    total = before_ref[...].astype(jnp.float32)
    for block in blocks:
        code = block[pl.ds(capacity, PAD), :].astype(jnp.float32)
        lines = [code[i : i + 1, :] for i in range(2 * pieces)]
        upper = lines[0] if pieces == 1 else jnp.concatenate(lines[:pieces], axis=1)
        lower = lines[1] if pieces == 1 else jnp.concatenate(lines[pieces:], axis=1)
        target = (8.0 * upper + lower).astype(jnp.int32)
        total += dot(sum_mask(target, rows16), block[pl.ds(0, capacity), :])
    out_ref[...] = total.astype(out_ref.dtype)


def gather_in(before, blocks, dtype, after=()):
    nodes, channels = before.shape
    slots = len(blocks) * blocks[0].shape[0]
    return call(
        functools.partial(gather_in_kernel, len(blocks)),
        [shape((nodes, channels), dtype)],
        [before, *blocks, *after],
        2 * nodes * slots * channels,
    )[0]


def sums_kernel(turn, target_ref, coef_ref, out_ref):
    rows16 = row_iota(out_ref.shape[0])
    for start in range(0, out_ref.shape[1], turn):
        here = pl.ds(start, turn)
        out_ref[:, here] = sum_mask(target_ref[:, here], rows16, coef_ref[:, here])


def edge_sums(m2m_dst, m2m_coef, nodes):
    edges = m2m_dst.shape[1]
    return call(
        functools.partial(sums_kernel, 512), [shape((nodes, edges))], [m2m_dst, m2m_coef], 4 * nodes * edges
    )[0]


def list_kernel(reach, listed_ref, state_ref, far_ref, near_ref, one_ref, two_ref):
    nodes = state_ref.shape[0]
    width = listed_ref.shape[2]
    lanes = lane_iota(nodes)
    region = lax.axis_index(REGION)
    core = region % 2
    wanted = [
        meets(region) - core + i - region for meets in (meets_two, meets_other_two) for i in range(2)
    ]
    wanted += [meets_other_three(region) - region, meets_core(region) - region]
    wanted = [offset + reach - jnp.where(offset > 0, 1, 0) for offset in wanted]
    for k in range(0, len(wanted), 2):
        row = jnp.concatenate([listed_ref[wanted[k + i]] for i in range(2)], axis=1)
        rows = dot(pick_mask(column(row).astype(jnp.int16), lanes), state_ref[...])
        rows = rows.astype(jnp.bfloat16)
        parts = [rows[i * width : (i + 1) * width] for i in range(2)]
        if k < 4:
            ref = one_ref if k == 0 else two_ref
            for i in range(2):
                ref[i] = parts[i]
        else:
            far_ref[pl.ds(0, width), :] = parts[0]
            far_ref[pl.ds(width, far_ref.shape[0] - width), :] = jnp.zeros(
                (far_ref.shape[0] - width, parts[0].shape[1]), jnp.bfloat16
            )
            near_ref[...] = parts[1]


def list_rows(state, halo_send, reach):
    nodes, channels = state.shape
    links, unused, width = halo_send.shape
    one, two = [shape(d) for d in ((width, channels), (2, width, channels))]
    far = shape((2 * width + PAD, channels))
    return call(
        functools.partial(list_kernel, reach),
        [far, one, two, two],
        [halo_send, state],
        0,
    )


def forward_kernel(distant_ref, near_ref, one_ref, two_ref, *refs):
    sent_ref, mine_ref = refs[-2:]
    width = near_ref.shape[0]
    core = lax.axis_index("edge")
    for k, part in enumerate((near_ref[...], one_ref[1 - core], two_ref[1 - core])):
        sent_ref[pl.ds(k * width, width), :] = part
    for k, part in enumerate((distant_ref[pl.ds(0, width), :], one_ref[core], two_ref[core])):
        mine_ref[pl.ds(k * width, width), :] = part


def exchange_listed(far, near, one, two, after):
    width, channels = near.shape
    distant = swapped(far, meets_other_three)
    one, two = swapped(one, meets_two), swapped(two, meets_other_two)
    half = shape((3 * width, channels))
    sent, mine = call(forward_kernel, [half, half], [distant, near, one, two, *after], 0)
    across = swapped(sent, meets_core)
    return [mine, *from_others(mine)], [across, *from_others(across)]


def ordered_rows(direct, across):
    width = direct.shape[0] // 3
    region = lax.axis_index(REGION)
    even = region % 2 == 0
    low_even = region // 2 % 2 == 0
    distant, *own = [direct[k * width : (k + 1) * width] for k in range(3)]
    near, *crossed = [across[k * width : (k + 1) * width] for k in range(3)]
    before, after = [
        [jnp.where(low_even == first, pair[0], pair[1]) for pair in (own, crossed)] for first in (False, True)
    ]
    rows = (
        jnp.where(even, after[1], distant),
        after[0],
        jnp.where(even, near, after[1]),
        jnp.where(even, before[1], near),
        before[0],
        jnp.where(even, distant, before[1]),
    )
    return jnp.concatenate(rows, axis=0)


def projected_rows(weight_ref, parts):
    weights = own_and_others_rows(weight_ref, parts[0].shape[1], len(parts) - 1)
    total = dot(parts[0][...], weights[0])
    for part, weight in zip(parts[1:], weights[1:]):
        total += dot(part[...], weight)
    return total.astype(jnp.bfloat16)


def project_kernel(layer, src_ref, dst_ref, *refs):
    states, table_ref = (refs[:-1], refs[-1])
    nodes = states[0].shape[0]
    table_ref[pl.ds(0, nodes), :] = projected_rows(src_ref.at[layer], states)
    table_ref[pl.ds(nodes, nodes), :] = projected_rows(dst_ref.at[layer], states)


def project(layer, states, src_weights, dst_weights):
    nodes, channels = states[0].shape
    depth = src_weights.shape[1]
    return call(
        functools.partial(project_kernel, layer),
        [shape((2 * nodes, channels))],
        [src_weights, dst_weights, *states],
        4 * nodes * depth * channels,
    )[0]


def first_kernel(turn, source_ref, target_ref, table_ref, out_ref):
    lanes = lane_iota(table_ref.shape[0] // 2)
    for start in range(0, source_ref.shape[0], turn):
        here = pl.ds(start, turn)
        mask = jnp.concatenate(
            [pick_mask(source_ref[here, :], lanes), pick_mask(target_ref[here, :], lanes)], axis=1
        )
        out_ref[here, :] = dot(mask, table_ref[...])


def first_part(source_col, target_col, table):
    rows, channels = table.shape
    edges = source_col.shape[0]
    return call(
        functools.partial(first_kernel, 512),
        [shape((edges, channels), jnp.float32)],
        [source_col, target_col, table],
        2 * edges * rows * channels,
    )[0]


def message_kernel(
    turn, turns, layer, source_ref, sums_ref, state_ref, first_ref, weight_ref, *refs
):
    listed, (out_ref, message_ref) = (refs[:-2], refs[-2:])
    nodes, channels = state_ref.shape
    half = len(listed) // 2
    table = ordered_rows(
        projected_rows(weight_ref.at[layer], listed[:half]), projected_rows(weight_ref.at[layer], listed[half:])
    )
    lanes = (lane_iota(table.shape[0]).astype(jnp.int32) + nodes).astype(jnp.int16)
    total = state_ref[...].astype(jnp.float32)
    edges = source_ref.shape[0]

    def gathered(start):
        here = pl.ds(start, turn)
        return first_ref[here, :] + dot(pick_mask(source_ref[here, :], lanes), table)

    ahead = gathered(0)
    for start in range(0, edges, turn):
        summed = ahead
        if start + turn < edges:
            ahead = gathered(start + turn)
        message_ref[pl.ds(start, turn), :] = silu(summed).astype(jnp.bfloat16)
        done = start // turn + 1
        if done % turns == 0:
            here = pl.ds((done - turns) * turn, turns * turn)
            total += dot(sums_ref[:, here], message_ref[here, :])
    out_ref[...] = total.astype(jnp.bfloat16)


def messages(layer, source_col, sums, state, first, src_weights, listed, final):
    nodes, channels = state.shape
    edges = source_col.shape[0]
    named = 2 * listed[0].shape[0]
    return call(
        functools.partial(message_kernel, 512, 5, layer),
        [shape((nodes, channels))],
        [source_col, sums, state, first, src_weights, *listed],
        2 * edges * (named + nodes) * channels,
        edges * channels,
        [pltpu.VMEM((edges, channels), jnp.bfloat16)],
        final,
    )[0]


def on_device(
    grid_latent,
    enc_weight,
    mesh_latent,
    g2m_src,
    g2m_dst,
    g2m_coef,
    src_weights,
    dst_weights,
    halo_send,
    m2m_src,
    m2m_dst,
    m2m_coef,
):
    reach = (g2m_src.shape[1] - 1) // 2
    assert reach == 3 and lax.axis_size("edge") == 2
    g2m_src, g2m_dst, g2m_coef, halo_send = [
        jnp.swapaxes(a, 0, 1) for a in (g2m_src, g2m_dst, g2m_coef, halo_send)
    ]
    groups = [
        (meets_other_three,), (meets_three,), (meets_two, meets_other_two), (meets_next, None), (meets_core,)
    ]
    picked, g2m_src, grid_latent = first_pick(groups[:2], g2m_src, grid_latent)
    arrived = [from_others(rows, group[0]) for group, rows in zip(groups, picked)]
    m2m_src, m2m_dst, m2m_coef, enc_weight, g2m_coef, g2m_dst, mesh_latent, halo_send, src_weights, dst_weights = (
        fetch(
            g2m_src, m2m_src, m2m_dst, m2m_coef, enc_weight, g2m_coef, g2m_dst, mesh_latent, halo_send,
            src_weights, dst_weights,
        )
    )
    source_col, target_col = cols = columns(m2m_src, m2m_dst)

    def pick_next(place, after):
        picked.extend(pick(groups[place : place + 1], g2m_src, grid_latent, after))
        arrived.append(from_others(picked[place]))

    def encode_group(place, after=()):
        return encode(groups[place], picked[place], arrived[place], enc_weight, g2m_coef, g2m_dst, after)

    pick_next(2, [*arrived[0], enc_weight])
    encoded = encode_group(0) + encode_group(1)
    pick_next(3, encoded)
    encoded += encode_group(2)
    blocks = [swapped(block, meets) for block, meets in zip(encoded, groups[0] + groups[1] + groups[2])]
    far_sum = gather_in(mesh_latent, blocks[:1], jnp.float32)
    state = gather_in(far_sum, blocks[1:2], jnp.float32)
    pick_next(4, [far_sum, *encoded[2:]])
    following, own = encode_group(3, [state])
    (near,) = encode_group(4)
    blocks.append(swapped(following, meets_next))
    near = swapped(near, meets_core)
    state = gather_in(state, blocks[2:4] + [own], jnp.float32, cols)
    state = gather_in(state, [blocks[4], near], jnp.bfloat16)
    sums = edge_sums(m2m_dst, m2m_coef, state.shape[0])
    layers = src_weights.shape[0]
    for layer in range(layers):
        others = from_others(state)
        direct, across = exchange_listed(*list_rows(state, halo_send, reach), [] if layer else [sums])
        table = project(layer, [state, *others], src_weights, dst_weights)
        first = first_part(source_col, target_col, table)
        state = messages(
            layer, source_col, sums, state, first, src_weights, direct + across, layer == layers - 1
        )
    return state


def solution(mesh):
    placed = (
        P(("groups", "space", "edge"), "feat"),
        P(None, "feat"),
        P(("groups", "space", "edge"), "feat"),
        P(("groups", "space", "edge"), None, None),
        P(("groups", "space", "edge"), None, None),
        P(("groups", "space", "edge"), None, None),
        P(None, None, "feat"),
        P(None, None, "feat"),
        P(("groups", "space", "edge"), None, None),
        P(("groups", "space", "edge"), None),
        P(("groups", "space", "edge"), None),
        P(("groups", "space", "edge"), None),
    )
    return jax.shard_map(
        on_device,
        mesh=mesh,
        in_specs=placed,
        out_specs=P(("groups", "space", "edge"), "feat"),
        check_vma=False,
    )
```
